32 devices in a mesh: dp: 4 (over y, x), gz: 8 (over z, core).
Axes of the slice: x: 2, y: 2, z: 4, core: 2. Of those that a mesh axis runs over, the one named last changes fastest.
Arguments:
- volume: bfloat16 [8, 4, 16, 2048], P('gz', 'dp'), may hold values from -6 to 6
- weight: bfloat16 [1728, 64], replicated, may hold values from -0.15625 to 0.15625
- cotangent: bfloat16 [8, 4, 16, 2048], P('gz', 'dp'), may hold values from -6 to 6
Outputs:
- activation: bfloat16 [8, 4, 16, 2048], P('gz', 'dp')
- input_grad: bfloat16 [8, 4, 16, 2048], P('gz', 'dp')
- weight_grad: float32 [1728, 64], P('gz', 'dp')
The draws below stay inside these ranges and needn't reach their ends.
All inputs are finite; a program needn't handle non-finite values.
Results may differ from the reference program's by a relative error of at most 0.01.
Values may be sent and summed in bfloat16 or wider, within the bound.
A program may use at most 64 MiB of HBM per device.

```python
import math
import jax
import jax.numpy as jnp
from jax import lax

C = 64
NH = 16
NW = 32
UNIVERSES = 8
NZ = 4


def levels(key, dims, cuts, least, top_value):
    loudness, own = 1.0, jax.random.fold_in(key, 6)
    for axis_at, parts in cuts:
        heights = jnp.exp(jax.random.uniform(jax.random.fold_in(own, axis_at), (parts,), jnp.float32, least / len(cuts), top_value / len(cuts)))
        loudness = loudness * jnp.repeat(heights, dims[axis_at] // parts).reshape([-1 if axis == axis_at else 1 for axis in range(len(dims))])
    return loudness


def scatter_about(stream_key, dims, width, limit, shards=(), held_as=jnp.bfloat16):
    drawn = jax.random.normal(stream_key, dims, jnp.float32) * width
    if len(shards) > 0:
        drawn = levels(stream_key, dims, shards, -0.22, 0.18) * drawn
    return jnp.clip(drawn, min=-limit, max=limit).astype(held_as)


def setup_inputs(seed: int = 0) -> dict:
    splits = jax.random.split(jax.random.key(seed), 4)
    volume = scatter_about(splits[0], (UNIVERSES, NZ, NH, NW * C), 1.0, 6.0, ((0, 8), (1, 4)))
    weight = scatter_about(splits[1], (27 * C, C), (27 * C) ** -0.5, 0.15625)
    cotangent = scatter_about(splits[2], (UNIVERSES, NZ, NH, NW * C), 1.0, 6.0, ((0, 8), (1, 4)))
    return {"volume": volume, "weight": weight, "cotangent": cotangent}


def reference(volume, weight, cotangent):
    kern = weight.astype(jnp.float32).reshape(3, 3, 3, C, C)
    hp = lax.Precision.HIGHEST

    def one_universe(pair):
        vol, cot = pair
        grid = vol.astype(jnp.float32).reshape(NZ, NH, NW, C)
        padded = jnp.pad(grid, ((1, 1), (1, 1), (1, 1), (0, 0)))
        pre = jnp.zeros((NZ * NH * NW, C), jnp.float32)
        for a in range(3):
            for b in range(3):
                for c in range(3):
                    window = padded[a:a + NZ, b:b + NH, c:c + NW].reshape(NZ * NH * NW, C)
                    pre = pre + jnp.dot(window, kern[a, b, c], precision=hp)
        sig = jax.nn.sigmoid(pre)
        act = (pre * sig).astype(jnp.bfloat16)
        delta_low = lax.optimization_barrier((cot.astype(jnp.float32).reshape(NZ * NH * NW, C) * sig * (1.0 + pre * (1.0 - sig))).astype(jnp.bfloat16))
        delta = delta_low.astype(jnp.float32)
        dpad = jnp.pad(delta.reshape(NZ, NH, NW, C), ((1, 1), (1, 1), (1, 1), (0, 0)))
        back = jnp.zeros((NZ * NH * NW, C), jnp.float32)
        grads = []
        for a in range(3):
            for b in range(3):
                for c in range(3):
                    window = dpad[2 - a:2 - a + NZ, 2 - b:2 - b + NH, 2 - c:2 - c + NW].reshape(NZ * NH * NW, C)
                    back = back + jnp.dot(window, kern[a, b, c].T, precision=hp)
                    source = padded[a:a + NZ, b:b + NH, c:c + NW].reshape(NZ * NH * NW, C)
                    grads.append(jnp.dot(source.T, delta, precision=hp))
        return (act.reshape(NZ, NH, NW * C), back.astype(jnp.bfloat16).reshape(NZ, NH, NW * C), jnp.stack(grads, 0))
    activation, input_grad, partial_grads = lax.map(one_universe, (volume, cotangent))
    scale = 1.0 / math.sqrt(UNIVERSES * NZ * NH * NW)
    weight_grad = lax.optimization_barrier(jnp.sum(partial_grads, 0)).reshape(27 * C, C) * scale
    return (activation, input_grad, weight_grad)
```

```python
import functools
import math

import jax
import jax.numpy as jnp
from jax import lax
from jax.experimental import pallas as pl
from jax.experimental.pallas import tpu as pltpu
from jax.sharding import PartitionSpec as P

MESH = pl.DeviceIdType.MESH
BF16 = jnp.bfloat16
F32 = jnp.float32


def rolled(x, shift, axis):
    return pltpu.roll(x, shift % x.shape[axis], axis)


def pair_rows(plane, height, pairs):
    return jnp.concatenate([plane[:, 128 * k : 128 * (k + 1)] for k in range(pairs)], axis=0)


def windows(plane, height, pairs):
    own = pair_rows(plane, height, pairs)
    zero = jnp.zeros((height, 128), own.dtype)
    after = jnp.concatenate([own[height:], zero], axis=0)
    before = jnp.concatenate([zero, own[:-height]], axis=0)
    lane = lax.broadcasted_iota(jnp.int32, own.shape, 1)
    return own, jnp.where(lane < 64, after, before)


def y_sum(parts, height):
    row = lax.broadcasted_iota(jnp.int32, (parts.shape[0], 128), 0) % height
    low = jnp.where(row == 0, 0.0, rolled(parts[:, 0:128], 1, 0))
    high = jnp.where(row == height - 1, 0.0, rolled(parts[:, 256:384], -1, 0))
    return parts[:, 128:256] + low + high


def kernel(
    geom, v_ref, w_ref, g_ref, act_ref, ig_ref, wg_ref,
    vbuf, gbuf, wbuf, dbuf, abuf, ibuf, win, dwin, wfwd, wbwd,
    send1, recv1, sum1, recv2, tall, wout,
    local_sem, vsend, vrecv, dsend, drecv, ssend1, srecv1, ssend2, srecv2,
):
    n, m, height, pairs, rows_out, cols_out, tiles, wide, scale = geom
    me = lax.axis_index("dp")
    my = lax.axis_index("gz")

    barrier = pltpu.get_barrier_semaphore()
    for k in range(1, n):
        pl.semaphore_signal(
            barrier, inc=1, device_id={"dp": lax.rem(me + k, n)}, device_id_type=MESH
        )
    for k in range(1, m):
        pl.semaphore_signal(
            barrier, inc=1, device_id={"gz": lax.rem(my + k, m)}, device_id_type=MESH
        )
    load_w = pltpu.make_async_copy(w_ref, wbuf, local_sem.at[0])
    load_v = pltpu.make_async_copy(v_ref.at[0, 0], vbuf.at[1], local_sem.at[1])
    load_g = pltpu.make_async_copy(g_ref.at[0, 0], gbuf, local_sem.at[2])
    load_w.start()
    load_v.start()
    load_g.start()
    pl.semaphore_wait(barrier, n + m - 2)

    def halo(source, buf, ssem, rsem):
        up = pltpu.make_async_remote_copy(
            src_ref=source, dst_ref=buf.at[0], send_sem=ssem.at[0], recv_sem=rsem.at[0],
            device_id={"dp": lax.rem(me + 1, n)}, device_id_type=MESH,
        )
        down = pltpu.make_async_remote_copy(
            src_ref=source, dst_ref=buf.at[2], send_sem=ssem.at[1], recv_sem=rsem.at[1],
            device_id={"dp": lax.rem(me + n - 1, n)}, device_id_type=MESH,
        )

        @pl.when(me < n - 1)
        def _():
            up.start()

        @pl.when(me > 0)
        def _():
            down.start()

        return up, down

    def halo_arrive(up, down, buf):
        @pl.when(me > 0)
        def _():
            up.wait_recv()

        @pl.when(me == 0)
        def _():
            buf[0] = jnp.zeros(buf.shape[1:], buf.dtype)

        @pl.when(me < n - 1)
        def _():
            down.wait_recv()

        @pl.when(me == n - 1)
        def _():
            buf[2] = jnp.zeros(buf.shape[1:], buf.dtype)

    def halo_sent(up, down):
        @pl.when(me < n - 1)
        def _():
            up.wait_send()

        @pl.when(me > 0)
        def _():
            down.wait_send()

    v_up, v_down = halo(v_ref.at[0, 0], vbuf, vsend, vrecv)

    load_w.wait()
    zero = jnp.zeros((64, 64), BF16)
    for a in range(3):
        for b in range(3):
            base = (a * 9 + b * 3) * 64
            k0, k1, k2 = (wbuf[base + 64 * c : base + 64 * (c + 1), :] for c in range(3))
            left = jnp.concatenate([k1, k2, zero, k0], axis=0)
            right = jnp.concatenate([k0, k1, k2, zero], axis=0)
            wfwd[256 * a : 256 * (a + 1), 128 * b : 128 * (b + 1)] = jnp.concatenate(
                [left, right], axis=1
            )
            top = jnp.concatenate([k1, k0, zero, k2], axis=1)
            bottom = jnp.concatenate([k2, k1, k0, zero], axis=1)
            fa, fb = 2 - a, 2 - b
            wbwd[128 * fb : 128 * (fb + 1), 256 * fa : 256 * (fa + 1)] = jnp.concatenate(
                [top, bottom], axis=0
            )

    def fill(target, buf, a):
        own, edge = windows(buf[a], height, pairs)
        target[:, 256 * a : 256 * a + 128] = own
        target[:, 256 * a + 128 : 256 * (a + 1)] = edge

    def plane_fwd(a):
        return jnp.dot(
            win[:, 256 * a : 256 * (a + 1)], wfwd[256 * a : 256 * (a + 1), :],
            preferred_element_type=F32,
        )

    load_v.wait()
    fill(win, vbuf, 1)
    parts = plane_fwd(1)
    load_g.wait()
    halo_arrive(v_up, v_down, vbuf)
    fill(win, vbuf, 0)
    fill(win, vbuf, 2)
    parts = parts + plane_fwd(0) + plane_fwd(2)
    pre = y_sum(parts, height)
    sig = 1.0 / (1.0 + jnp.exp(-pre))
    cot = pair_rows(gbuf[...], height, pairs).astype(F32)
    delta = (cot * sig * (1.0 + pre * (1.0 - sig))).astype(BF16)
    for k in range(pairs):
        dbuf[1, :, 128 * k : 128 * (k + 1)] = delta[height * k : height * (k + 1)]
    d_up, d_down = halo(dbuf.at[1], dbuf, dsend, drecv)

    wide_delta = delta.astype(F32)
    row = lax.broadcasted_iota(jnp.int32, wide_delta.shape, 0) % height
    ahead = jnp.where(row == height - 1, 0.0, rolled(wide_delta, -1, 0)).astype(BF16)
    behind = jnp.where(row == 0, 0.0, rolled(wide_delta, 1, 0)).astype(BF16)
    moved = jnp.concatenate([ahead, delta, behind], axis=1)
    lane = lax.broadcasted_iota(jnp.int32, (64, 128), 1) < 64
    terms = lax.dot_general(
        moved, win[...], (((0,), (0,)), ((), ())), preferred_element_type=F32
    )
    quads = []
    for q in range(9):
        a, b = q // 3, q % 3
        first = terms[128 * b : 128 * b + 64, 256 * a : 256 * (a + 1)]
        second = terms[128 * b + 64 : 128 * (b + 1), 256 * a : 256 * (a + 1)]
        quads.append((first[:, :128], first[:, 128:], second[:, :128], second[:, 128:]))
    out_tiles = []
    for q in range(0, 9, 2):
        a1, a2, b1, b2 = quads[q]
        out_tiles.append(rolled(jnp.where(lane, a1, a2), 64, 1) + b1)
        third = rolled(a1, 64, 1) + b2
        if q == 8:
            out_tiles.append(jnp.where(lane, third, 0.0))
            continue
        c1, c2, e1, e2 = quads[q + 1]
        out_tiles.append(jnp.where(lane, third, c2 + rolled(e1, 64, 1)))
        out_tiles.append(c1 + rolled(jnp.where(lane, e2, e1), 64, 1))
    for t in range(14):
        tile = (out_tiles[t] * scale).astype(BF16)
        for d in range(n):
            part = tile[cols_out * d : cols_out * (d + 1)]
            if cols_out % 16:
                part = jnp.concatenate(
                    [part, jnp.zeros((send1.shape[2] - cols_out, 128), BF16)], axis=0
                )
            send1[d, t] = part
    for d in range(n):
        for t in range(14, tiles):
            send1[d, t] = jnp.zeros(send1.shape[2:], BF16)
    first_copies = []
    for k in range(1, n):
        peer = lax.rem(me + k, n)
        copy = pltpu.make_async_remote_copy(
            src_ref=send1.at[peer], dst_ref=recv1.at[k - 1],
            send_sem=ssend1.at[k - 1], recv_sem=srecv1.at[k - 1],
            device_id={"dp": peer}, device_id_type=MESH,
        )
        copy.start()
        first_copies.append(copy)

    act = (pre * sig).astype(BF16)
    for k in range(pairs):
        abuf[:, 128 * k : 128 * (k + 1)] = act[height * k : height * (k + 1)]
    store_a = pltpu.make_async_copy(abuf, act_ref.at[0, 0], local_sem.at[0])
    store_a.start()

    halo_arrive(d_up, d_down, dbuf)
    for a in range(3):
        fill(dwin, dbuf, a)
    back = lax.dot_general(
        dwin[...], wbwd[...], (((1,), (1,)), ((), ())), preferred_element_type=F32
    )
    grad = y_sum(back, height).astype(BF16)
    for k in range(pairs):
        ibuf[:, 128 * k : 128 * (k + 1)] = grad[height * k : height * (k + 1)]
    store_i = pltpu.make_async_copy(ibuf, ig_ref.at[0, 0], local_sem.at[1])
    store_i.start()

    total = send1[me].astype(F32)
    for k in range(1, n):
        first_copies[k - 1].wait_recv()
        total = total + recv1[k - 1].astype(F32)
    sum1[...] = total.astype(BF16)
    second_copies = []
    for k in range(1, m):
        peer = lax.rem(my + k, m)
        copy = pltpu.make_async_remote_copy(
            src_ref=sum1.at[pl.ds((peer * rows_out) // 128, wide)], dst_ref=recv2.at[k - 1],
            send_sem=ssend2.at[k - 1], recv_sem=srecv2.at[k - 1],
            device_id={"gz": peer}, device_id_type=MESH,
        )
        copy.start()
        second_copies.append(copy)
    halo_sent(v_up, v_down)
    halo_sent(d_up, d_down)
    for copy in first_copies:
        copy.wait_send()
    store_a.wait()
    store_i.wait()
    total = sum1[pl.ds((my * rows_out) // 128, wide)].astype(F32)
    for k in range(1, m):
        second_copies[k - 1].wait_recv()
        total = total + recv2[k - 1].astype(F32)
    for t in range(wide):
        tall[128 * t : 128 * (t + 1), :] = total[t].T
    wout[...] = tall[pl.ds(lax.rem(my * rows_out, 128), rows_out), :][:, :cols_out]
    store_w = pltpu.make_async_copy(wout, wg_ref, local_sem.at[2])
    store_w.start()
    for copy in second_copies:
        copy.wait_send()
    store_w.wait()


def per_device(volume, weight, cotangent):
    n = lax.axis_size("dp")
    m = lax.axis_size("gz")
    chans = weight.shape[1]
    universes, planes, height, merged = volume.shape
    assert chans == 64 and universes == 1 and planes == 1
    pairs = merged // 128
    cells = height * pairs * 2
    rows_out = weight.shape[0] // m
    cols_out = chans // n
    padded = -(-cols_out // 16) * 16
    wide = max(-(-((g * rows_out) % 128 + rows_out) // 128) for g in range(m))
    tiles = max(14, max((g * rows_out) // 128 + wide for g in range(m)))
    scale = 1.0 / math.sqrt(n * m * cells)
    geom = (n, m, height, pairs, rows_out, cols_out, tiles, wide, scale)
    vmem = pltpu.VMEM
    dma = pltpu.SemaphoreType.DMA
    block = (height, merged)
    grid_rows = pairs * height
    return pl.pallas_call(
        functools.partial(kernel, geom),
        out_shape=(
            jax.ShapeDtypeStruct(volume.shape, BF16),
            jax.ShapeDtypeStruct(volume.shape, BF16),
            jax.ShapeDtypeStruct((rows_out, cols_out), F32),
        ),
        in_specs=[pl.BlockSpec(memory_space=pl.ANY)] * 3,
        out_specs=[pl.BlockSpec(memory_space=pl.ANY)] * 3,
        scratch_shapes=[
            vmem((3, *block), BF16),
            vmem(block, BF16),
            vmem(weight.shape, BF16),
            vmem((3, *block), BF16),
            vmem(block, BF16),
            vmem(block, BF16),
            vmem((grid_rows, 768), BF16),
            vmem((grid_rows, 768), BF16),
            vmem((768, 384), BF16),
            vmem((384, 768), BF16),
            vmem((n, tiles, padded, 128), BF16),
            vmem((n - 1, tiles, padded, 128), BF16),
            vmem((tiles, padded, 128), BF16),
            vmem((m - 1, wide, padded, 128), BF16),
            vmem((wide * 128, padded), F32),
            vmem((rows_out, cols_out), F32),
            dma((3,)), dma((2,)), dma((2,)), dma((2,)), dma((2,)),
            dma((n - 1,)), dma((n - 1,)), dma((m - 1,)), dma((m - 1,)),
        ],
        compiler_params=pltpu.CompilerParams(
            collective_id=0, has_side_effects=True, vmem_limit_bytes=32 * 1024 * 1024
        ),
    )(volume, weight, cotangent)


def solution(mesh):
    return jax.shard_map(
        per_device,
        mesh=mesh,
        in_specs=(P("gz", "dp", None, None), P(), P("gz", "dp", None, None)),
        out_specs=(P("gz", "dp", None, None), P("gz", "dp", None, None), P("gz", "dp")),
        check_vma=False,
    )
```

```python
import functools
import math

import jax
import jax.numpy as jnp
from jax import lax
from jax.experimental import pallas as pl
from jax.experimental.pallas import tpu as pltpu
from jax.sharding import PartitionSpec as P

MESH = pl.DeviceIdType.MESH
BF16 = jnp.bfloat16
F32 = jnp.float32


def rolled(x, shift, axis):
    return pltpu.roll(x, shift % x.shape[axis], axis)


def pair_rows(plane, height, pairs):
    return jnp.concatenate([plane[:, 128 * k : 128 * (k + 1)] for k in range(pairs)], axis=0)


def windows(plane, height, pairs):
    own = pair_rows(plane, height, pairs)
    zero = jnp.zeros((height, 128), own.dtype)
    after = jnp.concatenate([own[height:], zero], axis=0)
    before = jnp.concatenate([zero, own[:-height]], axis=0)
    lane = lax.broadcasted_iota(jnp.int32, own.shape, 1)
    return own, jnp.where(lane < 64, after, before)


def y_sum(parts, height):
    row = lax.broadcasted_iota(jnp.int32, (parts.shape[0], 128), 0) % height
    low = jnp.where(row == 0, 0.0, rolled(parts[:, 0:128], 1, 0))
    high = jnp.where(row == height - 1, 0.0, rolled(parts[:, 256:384], -1, 0))
    return parts[:, 128:256] + low + high


def kernel(
    geom, v_ref, w_ref, g_ref, act_ref, ig_ref, wg_ref,
    vbuf, gbuf, wbuf, dbuf, abuf, ibuf, win, dwin, wfwd, wbwd,
    send1, recv1, sum1, recv2, wout,
    local_sem, vsend, vrecv, dsend, drecv, ssend1, srecv1, ssend2, srecv2,
):
    n, m, height, pairs, rows_out, cols_out, tiles, wide, scale = geom
    me = lax.axis_index("dp")
    my = lax.axis_index("gz")

    barrier = pltpu.get_barrier_semaphore()
    for k in range(1, n):
        pl.semaphore_signal(
            barrier, inc=1, device_id={"dp": lax.rem(me + k, n)}, device_id_type=MESH
        )
    for k in range(1, m):
        pl.semaphore_signal(
            barrier, inc=1, device_id={"gz": lax.rem(my + k, m)}, device_id_type=MESH
        )
    load_w = pltpu.make_async_copy(w_ref, wbuf, local_sem.at[0])
    load_v = pltpu.make_async_copy(v_ref.at[0, 0], vbuf.at[1], local_sem.at[1])
    load_g = pltpu.make_async_copy(g_ref.at[0, 0], gbuf, local_sem.at[2])
    load_w.start()
    load_v.start()
    load_g.start()
    pl.semaphore_wait(barrier, n + m - 2)

    def halo(source, buf, ssem, rsem):
        up = pltpu.make_async_remote_copy(
            src_ref=source, dst_ref=buf.at[0], send_sem=ssem.at[0], recv_sem=rsem.at[0],
            device_id={"dp": lax.rem(me + 1, n)}, device_id_type=MESH,
        )
        down = pltpu.make_async_remote_copy(
            src_ref=source, dst_ref=buf.at[2], send_sem=ssem.at[1], recv_sem=rsem.at[1],
            device_id={"dp": lax.rem(me + n - 1, n)}, device_id_type=MESH,
        )

        @pl.when(me < n - 1)
        def _():
            up.start()

        @pl.when(me > 0)
        def _():
            down.start()

        return up, down

    def halo_arrive(up, down, buf):
        @pl.when(me > 0)
        def _():
            up.wait_recv()

        @pl.when(me == 0)
        def _():
            buf[0] = jnp.zeros(buf.shape[1:], buf.dtype)

        @pl.when(me < n - 1)
        def _():
            down.wait_recv()

        @pl.when(me == n - 1)
        def _():
            buf[2] = jnp.zeros(buf.shape[1:], buf.dtype)

    def halo_sent(up, down):
        @pl.when(me < n - 1)
        def _():
            up.wait_send()

        @pl.when(me > 0)
        def _():
            down.wait_send()

    v_up, v_down = halo(v_ref.at[0, 0], vbuf, vsend, vrecv)

    load_w.wait()
    zero = jnp.zeros((64, 64), BF16)
    for a in range(3):
        for b in range(3):
            base = (a * 9 + b * 3) * 64
            k0, k1, k2 = (wbuf[:, base + 64 * c : base + 64 * (c + 1)] for c in range(3))
            top = jnp.concatenate([k1, k2, zero, k0], axis=1)
            bottom = jnp.concatenate([k0, k1, k2, zero], axis=1)
            wfwd[128 * b : 128 * (b + 1), 256 * a : 256 * (a + 1)] = jnp.concatenate(
                [top, bottom], axis=0
            )
            left = jnp.concatenate([k1, k0, zero, k2], axis=0)
            right = jnp.concatenate([k2, k1, k0, zero], axis=0)
            fa, fb = 2 - a, 2 - b
            wbwd[256 * fa : 256 * (fa + 1), 128 * fb : 128 * (fb + 1)] = jnp.concatenate(
                [left, right], axis=1
            )

    def fill(target, buf, a):
        own, edge = windows(buf[a], height, pairs)
        target[:, 256 * a : 256 * a + 128] = own
        target[:, 256 * a + 128 : 256 * (a + 1)] = edge

    def plane_fwd(a):
        return lax.dot_general(
            win[:, 256 * a : 256 * (a + 1)], wfwd[:, 256 * a : 256 * (a + 1)],
            (((1,), (1,)), ((), ())), preferred_element_type=F32,
        )

    load_v.wait()
    fill(win, vbuf, 1)
    parts = plane_fwd(1)
    load_g.wait()
    halo_arrive(v_up, v_down, vbuf)
    fill(win, vbuf, 0)
    fill(win, vbuf, 2)
    parts = parts + plane_fwd(0) + plane_fwd(2)
    pre = y_sum(parts, height)
    sig = 1.0 / (1.0 + jnp.exp(-pre))
    cot = pair_rows(gbuf[...], height, pairs).astype(F32)
    delta = (cot * sig * (1.0 + pre * (1.0 - sig))).astype(BF16)
    for k in range(pairs):
        dbuf[1, :, 128 * k : 128 * (k + 1)] = delta[height * k : height * (k + 1)]
    d_up, d_down = halo(dbuf.at[1], dbuf, dsend, drecv)

    wide_delta = delta.astype(F32)
    row = lax.broadcasted_iota(jnp.int32, wide_delta.shape, 0) % height
    ahead = jnp.where(row == height - 1, 0.0, rolled(wide_delta, -1, 0)).astype(BF16)
    behind = jnp.where(row == 0, 0.0, rolled(wide_delta, 1, 0)).astype(BF16)
    moved = jnp.concatenate([ahead, delta, behind], axis=1)
    lane = lax.broadcasted_iota(jnp.int32, (64, 128), 1) < 64
    terms = lax.dot_general(
        moved, win[...], (((0,), (0,)), ((), ())), preferred_element_type=F32
    )
    quads = []
    for q in range(9):
        a, b = q // 3, q % 3
        first = terms[128 * b : 128 * b + 64, 256 * a : 256 * (a + 1)]
        second = terms[128 * b + 64 : 128 * (b + 1), 256 * a : 256 * (a + 1)]
        quads.append((first[:, :128], first[:, 128:], second[:, :128], second[:, 128:]))
    out_tiles = []
    for q in range(0, 9, 2):
        a1, a2, b1, b2 = quads[q]
        out_tiles.append(rolled(jnp.where(lane, a1, a2), 64, 1) + b1)
        third = rolled(a1, 64, 1) + b2
        if q == 8:
            out_tiles.append(jnp.where(lane, third, 0.0))
            continue
        c1, c2, e1, e2 = quads[q + 1]
        out_tiles.append(jnp.where(lane, third, c2 + rolled(e1, 64, 1)))
        out_tiles.append(c1 + rolled(jnp.where(lane, e2, e1), 64, 1))
    for t in range(14):
        tile = (out_tiles[t] * scale).astype(BF16)
        for d in range(n):
            part = tile[cols_out * d : cols_out * (d + 1)]
            if cols_out % 16:
                part = jnp.concatenate(
                    [part, jnp.zeros((send1.shape[2] - cols_out, 128), BF16)], axis=0
                )
            send1[d, t] = part
    for d in range(n):
        for t in range(14, tiles):
            send1[d, t] = jnp.zeros(send1.shape[2:], BF16)
    first_copies = []
    for k in range(1, n):
        peer = lax.rem(me + k, n)
        copy = pltpu.make_async_remote_copy(
            src_ref=send1.at[peer], dst_ref=recv1.at[k - 1],
            send_sem=ssend1.at[k - 1], recv_sem=srecv1.at[k - 1],
            device_id={"dp": peer}, device_id_type=MESH,
        )
        copy.start()
        first_copies.append(copy)

    act = (pre * sig).astype(BF16)
    for k in range(pairs):
        abuf[:, 128 * k : 128 * (k + 1)] = act[height * k : height * (k + 1)]
    store_a = pltpu.make_async_copy(abuf, act_ref.at[0, 0], local_sem.at[0])
    store_a.start()

    halo_arrive(d_up, d_down, dbuf)
    for a in range(3):
        fill(dwin, dbuf, a)
    back = jnp.dot(dwin[...], wbwd[...], preferred_element_type=F32)
    grad = y_sum(back, height).astype(BF16)
    for k in range(pairs):
        ibuf[:, 128 * k : 128 * (k + 1)] = grad[height * k : height * (k + 1)]
    store_i = pltpu.make_async_copy(ibuf, ig_ref.at[0, 0], local_sem.at[1])
    store_i.start()

    total = send1[me].astype(F32)
    for k in range(1, n):
        first_copies[k - 1].wait_recv()
        total = total + recv1[k - 1].astype(F32)
    sum1[...] = total.astype(BF16)
    second_copies = []
    for k in range(1, m):
        peer = lax.rem(my + k, m)
        copy = pltpu.make_async_remote_copy(
            src_ref=sum1.at[pl.ds((peer * rows_out) // 128, wide)], dst_ref=recv2.at[k - 1],
            send_sem=ssend2.at[k - 1], recv_sem=srecv2.at[k - 1],
            device_id={"gz": peer}, device_id_type=MESH,
        )
        copy.start()
        second_copies.append(copy)
    halo_sent(v_up, v_down)
    halo_sent(d_up, d_down)
    for copy in first_copies:
        copy.wait_send()
    store_a.wait()
    store_i.wait()
    total = sum1[pl.ds((my * rows_out) // 128, wide)].astype(F32)
    for k in range(1, m):
        second_copies[k - 1].wait_recv()
        total = total + recv2[k - 1].astype(F32)
    offset = lax.rem(my * rows_out, 128)
    lane = lax.broadcasted_iota(jnp.int32, total.shape[1:], 1)
    turned = [pltpu.roll(total[t], lax.rem(128 - offset, 128), 1) for t in range(wide)]
    for t in range(-(-rows_out // 128)):
        count = min(128, rows_out - 128 * t)
        after = turned[min(t + 1, wide - 1)]
        tile = jnp.where(lane < 128 - offset, turned[t], after)
        wout[:, 128 * t : 128 * t + count] = tile[:cols_out, :count]
    store_w = pltpu.make_async_copy(wout, wg_ref, local_sem.at[2])
    store_w.start()
    for copy in second_copies:
        copy.wait_send()
    store_w.wait()


def place(a_ref, i_ref, w_ref, act_ref, ig_ref, wg_ref, sem):
    pairs = ((a_ref, act_ref), (i_ref, ig_ref), (w_ref, wg_ref))
    copies = [pltpu.make_async_copy(a, b, sem.at[k]) for k, (a, b) in enumerate(pairs)]
    for copy in copies:
        copy.start()
    for copy in copies:
        copy.wait()


def per_device(volume, weight, cotangent):
    n = lax.axis_size("dp")
    m = lax.axis_size("gz")
    chans = weight.shape[1]
    universes, planes, height, merged = volume.shape
    assert chans == 64 and universes == 1 and planes == 1
    pairs = merged // 128
    cells = height * pairs * 2
    rows_out = weight.shape[0] // m
    cols_out = chans // n
    padded = -(-cols_out // 16) * 16
    wide = max(-(-((g * rows_out) % 128 + rows_out) // 128) for g in range(m))
    tiles = max(14, max((g * rows_out) // 128 + wide for g in range(m)))
    scale = 1.0 / math.sqrt(n * m * cells)
    geom = (n, m, height, pairs, rows_out, cols_out, tiles, wide, scale)
    vmem = pltpu.VMEM
    dma = pltpu.SemaphoreType.DMA
    block = (height, merged)
    grid_rows = pairs * height
    results = pl.pallas_call(
        functools.partial(kernel, geom),
        out_shape=(
            jax.ShapeDtypeStruct(volume.shape, BF16),
            jax.ShapeDtypeStruct(volume.shape, BF16),
            jax.ShapeDtypeStruct((cols_out, rows_out), F32),
        ),
        in_specs=[pl.BlockSpec(memory_space=pltpu.HBM)] * 3,
        out_specs=[pl.BlockSpec(memory_space=pl.ANY)] * 3,
        scratch_shapes=[
            vmem((3, *block), BF16),
            vmem(block, BF16),
            vmem(weight.shape[::-1], BF16),
            vmem((3, *block), BF16),
            vmem(block, BF16),
            vmem(block, BF16),
            vmem((grid_rows, 768), BF16),
            vmem((grid_rows, 768), BF16),
            vmem((384, 768), BF16),
            vmem((768, 384), BF16),
            vmem((n, tiles, padded, 128), BF16),
            vmem((n - 1, tiles, padded, 128), BF16),
            vmem((tiles, padded, 128), BF16),
            vmem((m - 1, wide, padded, 128), BF16),
            vmem((cols_out, rows_out), F32),
            dma((3,)), dma((2,)), dma((2,)), dma((2,)), dma((2,)),
            dma((n - 1,)), dma((n - 1,)), dma((m - 1,)), dma((m - 1,)),
        ],
        compiler_params=pltpu.CompilerParams(
            collective_id=0, has_side_effects=True, vmem_limit_bytes=63 * 1024 * 1024
        ),
    )(volume, weight.T, cotangent)
    activation, input_grad, weight_grad = pl.pallas_call(
        place,
        out_shape=tuple(jax.ShapeDtypeStruct(r.shape, r.dtype) for r in results),
        in_specs=[pl.BlockSpec(memory_space=pl.ANY)] * 3,
        out_specs=[pl.BlockSpec(memory_space=pl.ANY)] * 3,
        scratch_shapes=[dma((3,))],
        compiler_params=pltpu.CompilerParams(vmem_limit_bytes=63 * 1024 * 1024),
    )(*results)
    return activation, input_grad, weight_grad.T


def solution(mesh):
    return jax.shard_map(
        per_device,
        mesh=mesh,
        in_specs=(P("gz", "dp", None, None), P(), P("gz", "dp", None, None)),
        out_specs=(P("gz", "dp", None, None), P("gz", "dp", None, None), P("gz", "dp")),
        check_vma=False,
    )
```

```python
import functools
import math

import jax
import jax.numpy as jnp
from jax import lax
from jax.experimental import pallas as pl
from jax.experimental.pallas import tpu as pltpu
from jax.sharding import PartitionSpec as P

MESH = pl.DeviceIdType.MESH
BF16 = jnp.bfloat16
F32 = jnp.float32


def rolled(x, shift, axis):
    return pltpu.roll(x, shift % x.shape[axis], axis)


def pair_rows(plane, height, pairs):
    return jnp.concatenate([plane[:, 128 * k : 128 * (k + 1)] for k in range(pairs)], axis=0)


def windows(plane, height, pairs):
    own = pair_rows(plane, height, pairs)
    zero = jnp.zeros((height, 128), own.dtype)
    after = jnp.concatenate([own[height:], zero], axis=0)
    before = jnp.concatenate([zero, own[:-height]], axis=0)
    lane = lax.broadcasted_iota(jnp.int32, own.shape, 1)
    return own, jnp.where(lane < 64, after, before)


def y_sum(parts, height):
    row = lax.broadcasted_iota(jnp.int32, (parts.shape[0], 128), 0) % height
    low = jnp.where(row == 0, 0.0, rolled(parts[:, 0:128], 1, 0))
    high = jnp.where(row == height - 1, 0.0, rolled(parts[:, 256:384], -1, 0))
    return parts[:, 128:256] + low + high


def kernel(
    geom, v_ref, w_ref, g_ref, act_ref, ig_ref, wg_ref,
    vbuf, gbuf, wbuf, dbuf, win, dwin, wfwd, wbwd,
    send1, recv1, sum1, recv2,
    local_sem, vsend, vrecv, dsend, drecv, ssend1, srecv1, ssend2, srecv2,
):
    n, m, height, pairs, rows_out, cols_out, tiles, wide, scale = geom
    me = lax.axis_index("dp")
    my = lax.axis_index("gz")

    barrier = pltpu.get_barrier_semaphore()
    for k in range(1, n):
        pl.semaphore_signal(
            barrier, inc=1, device_id={"dp": lax.rem(me + k, n)}, device_id_type=MESH
        )
    for k in range(1, m):
        pl.semaphore_signal(
            barrier, inc=1, device_id={"gz": lax.rem(my + k, m)}, device_id_type=MESH
        )
    load_w = pltpu.make_async_copy(w_ref, wbuf, local_sem.at[0])
    load_v = pltpu.make_async_copy(v_ref.at[0, 0], vbuf.at[1], local_sem.at[1])
    load_g = pltpu.make_async_copy(g_ref.at[0, 0], gbuf, local_sem.at[2])
    load_w.start()
    load_v.start()
    load_g.start()
    pl.semaphore_wait(barrier, n + m - 2)

    def halo(source, buf, ssem, rsem):
        up = pltpu.make_async_remote_copy(
            src_ref=source, dst_ref=buf.at[0], send_sem=ssem.at[0], recv_sem=rsem.at[0],
            device_id={"dp": lax.rem(me + 1, n)}, device_id_type=MESH,
        )
        down = pltpu.make_async_remote_copy(
            src_ref=source, dst_ref=buf.at[2], send_sem=ssem.at[1], recv_sem=rsem.at[1],
            device_id={"dp": lax.rem(me + n - 1, n)}, device_id_type=MESH,
        )

        @pl.when(me < n - 1)
        def _():
            up.start()

        @pl.when(me > 0)
        def _():
            down.start()

        return up, down

    def halo_arrive(up, down, buf):
        @pl.when(me > 0)
        def _():
            up.wait_recv()

        @pl.when(me == 0)
        def _():
            buf[0] = jnp.zeros(buf.shape[1:], buf.dtype)

        @pl.when(me < n - 1)
        def _():
            down.wait_recv()

        @pl.when(me == n - 1)
        def _():
            buf[2] = jnp.zeros(buf.shape[1:], buf.dtype)

    def halo_sent(up, down):
        @pl.when(me < n - 1)
        def _():
            up.wait_send()

        @pl.when(me > 0)
        def _():
            down.wait_send()

    v_up, v_down = halo(v_ref.at[0, 0], vbuf, vsend, vrecv)

    load_w.wait()
    zero = jnp.zeros((64, 64), BF16)
    for a in range(3):
        for b in range(3):
            base = (a * 9 + b * 3) * 64
            k0, k1, k2 = (wbuf[:, base + 64 * c : base + 64 * (c + 1)] for c in range(3))
            top = jnp.concatenate([k1, k2, zero, k0], axis=1)
            bottom = jnp.concatenate([k0, k1, k2, zero], axis=1)
            wfwd[128 * b : 128 * (b + 1), 256 * a : 256 * (a + 1)] = jnp.concatenate(
                [top, bottom], axis=0
            )
            left = jnp.concatenate([k1, k0, zero, k2], axis=0)
            right = jnp.concatenate([k2, k1, k0, zero], axis=0)
            fa, fb = 2 - a, 2 - b
            wbwd[256 * fa : 256 * (fa + 1), 128 * fb : 128 * (fb + 1)] = jnp.concatenate(
                [left, right], axis=1
            )

    def fill(target, buf, a):
        own, edge = windows(buf[a], height, pairs)
        target[:, 256 * a : 256 * a + 128] = own
        target[:, 256 * a + 128 : 256 * (a + 1)] = edge

    def plane_fwd(a):
        return lax.dot_general(
            win[:, 256 * a : 256 * (a + 1)], wfwd[:, 256 * a : 256 * (a + 1)],
            (((1,), (1,)), ((), ())), preferred_element_type=F32,
        )

    load_v.wait()
    fill(win, vbuf, 1)
    parts = plane_fwd(1)
    load_g.wait()
    halo_arrive(v_up, v_down, vbuf)
    fill(win, vbuf, 0)
    fill(win, vbuf, 2)
    parts = parts + plane_fwd(0) + plane_fwd(2)
    pre = y_sum(parts, height)
    sig = 1.0 / (1.0 + jnp.exp(-pre))
    cot = pair_rows(gbuf[...], height, pairs).astype(F32)
    delta = (cot * sig * (1.0 + pre * (1.0 - sig))).astype(BF16)
    for k in range(pairs):
        dbuf[1, :, 128 * k : 128 * (k + 1)] = delta[height * k : height * (k + 1)]

    wide_delta = delta.astype(F32)
    row = lax.broadcasted_iota(jnp.int32, wide_delta.shape, 0) % height
    ahead = jnp.where(row == height - 1, 0.0, rolled(wide_delta, -1, 0)).astype(BF16)
    behind = jnp.where(row == 0, 0.0, rolled(wide_delta, 1, 0)).astype(BF16)
    moved = jnp.concatenate([ahead, delta, behind], axis=1)
    lane = lax.broadcasted_iota(jnp.int32, (64, 128), 1) < 64
    terms = lax.dot_general(
        moved, win[...], (((0,), (0,)), ((), ())), preferred_element_type=F32
    )
    quads = []
    for q in range(9):
        a, b = q // 3, q % 3
        first = terms[128 * b : 128 * b + 64, 256 * a : 256 * (a + 1)]
        second = terms[128 * b + 64 : 128 * (b + 1), 256 * a : 256 * (a + 1)]
        quads.append((first[:, :128], first[:, 128:], second[:, :128], second[:, 128:]))
    out_tiles = []
    for q in range(0, 9, 2):
        a1, a2, b1, b2 = quads[q]
        out_tiles.append(rolled(jnp.where(lane, a1, a2), 64, 1) + b1)
        third = rolled(a1, 64, 1) + b2
        if q == 8:
            out_tiles.append(jnp.where(lane, third, 0.0))
            continue
        c1, c2, e1, e2 = quads[q + 1]
        out_tiles.append(jnp.where(lane, third, c2 + rolled(e1, 64, 1)))
        out_tiles.append(c1 + rolled(jnp.where(lane, e2, e1), 64, 1))
    for t in range(14):
        tile = (out_tiles[t] * scale).astype(BF16)
        for d in range(n):
            part = tile[cols_out * d : cols_out * (d + 1)]
            if cols_out % 16:
                part = jnp.concatenate(
                    [part, jnp.zeros((send1.shape[2] - cols_out, 128), BF16)], axis=0
                )
            send1[d, t] = part
    for d in range(n):
        for t in range(14, tiles):
            send1[d, t] = jnp.zeros(send1.shape[2:], BF16)
    first_copies = []
    for k in range(1, n):
        peer = lax.rem(me + k, n)
        copy = pltpu.make_async_remote_copy(
            src_ref=send1.at[peer], dst_ref=recv1.at[k - 1],
            send_sem=ssend1.at[k - 1], recv_sem=srecv1.at[k - 1],
            device_id={"dp": peer}, device_id_type=MESH,
        )
        copy.start()
        first_copies.append(copy)

    d_up, d_down = halo(dbuf.at[1], dbuf, dsend, drecv)

    act = (pre * sig).astype(BF16)
    for k in range(pairs):
        act_ref[0, 0, :, 128 * k : 128 * (k + 1)] = act[height * k : height * (k + 1)]

    total = send1[me].astype(F32)
    for k in range(1, n):
        first_copies[k - 1].wait_recv()
        total = total + recv1[k - 1].astype(F32)
    sum1[...] = total.astype(BF16)
    second_copies = []
    for k in range(1, m):
        peer = lax.rem(my + k, m)
        copy = pltpu.make_async_remote_copy(
            src_ref=sum1.at[pl.ds((peer * rows_out) // 128, wide)], dst_ref=recv2.at[k - 1],
            send_sem=ssend2.at[k - 1], recv_sem=srecv2.at[k - 1],
            device_id={"gz": peer}, device_id_type=MESH,
        )
        copy.start()
        second_copies.append(copy)
    halo_arrive(d_up, d_down, dbuf)
    for a in range(3):
        fill(dwin, dbuf, a)
    back = jnp.dot(dwin[...], wbwd[...], preferred_element_type=F32)
    grad = y_sum(back, height).astype(BF16)
    for k in range(pairs):
        ig_ref[0, 0, :, 128 * k : 128 * (k + 1)] = grad[height * k : height * (k + 1)]

    halo_sent(v_up, v_down)
    halo_sent(d_up, d_down)
    for copy in first_copies:
        copy.wait_send()
    total = sum1[pl.ds((my * rows_out) // 128, wide)].astype(F32)
    for k in range(1, m):
        second_copies[k - 1].wait_recv()
        total = total + recv2[k - 1].astype(F32)
    offset = lax.rem(my * rows_out, 128)
    lane = lax.broadcasted_iota(jnp.int32, total.shape[1:], 1)
    turned = [pltpu.roll(total[t], lax.rem(128 - offset, 128), 1) for t in range(wide)]
    for t in range(-(-rows_out // 128)):
        count = min(128, rows_out - 128 * t)
        after = turned[min(t + 1, wide - 1)]
        tile = jnp.where(lane < 128 - offset, turned[t], after)
        wg_ref[:, 128 * t : 128 * t + count] = tile[:cols_out, :count]
    for copy in second_copies:
        copy.wait_send()


def place(a_ref, i_ref, w_ref, act_ref, ig_ref, wg_ref, sem):
    pairs = ((a_ref, act_ref), (i_ref, ig_ref), (w_ref, wg_ref))
    copies = [pltpu.make_async_copy(a, b, sem.at[k]) for k, (a, b) in enumerate(pairs)]
    for copy in copies:
        copy.start()
    for copy in copies:
        copy.wait()


def per_device(volume, weight, cotangent):
    n = lax.axis_size("dp")
    m = lax.axis_size("gz")
    chans = weight.shape[1]
    universes, planes, height, merged = volume.shape
    assert chans == 64 and universes == 1 and planes == 1
    pairs = merged // 128
    cells = height * pairs * 2
    rows_out = weight.shape[0] // m
    cols_out = chans // n
    padded = -(-cols_out // 16) * 16
    wide = max(-(-((g * rows_out) % 128 + rows_out) // 128) for g in range(m))
    tiles = max(14, max((g * rows_out) // 128 + wide for g in range(m)))
    scale = 1.0 / math.sqrt(n * m * cells)
    geom = (n, m, height, pairs, rows_out, cols_out, tiles, wide, scale)
    vmem = pltpu.VMEM
    dma = pltpu.SemaphoreType.DMA
    block = (height, merged)
    grid_rows = pairs * height
    results = pl.pallas_call(
        functools.partial(kernel, geom),
        out_shape=(
            vmem(volume.shape, BF16),
            vmem(volume.shape, BF16),
            vmem((cols_out, rows_out), F32),
        ),
        in_specs=[pl.BlockSpec(memory_space=pltpu.HBM)] * 3,
        out_specs=[pl.BlockSpec(memory_space=pltpu.VMEM)] * 3,
        scratch_shapes=[
            vmem((3, *block), BF16),
            vmem(block, BF16),
            vmem(weight.shape[::-1], BF16),
            vmem((3, *block), BF16),
            vmem((grid_rows, 768), BF16),
            vmem((grid_rows, 768), BF16),
            vmem((384, 768), BF16),
            vmem((768, 384), BF16),
            vmem((n, tiles, padded, 128), BF16),
            vmem((n - 1, tiles, padded, 128), BF16),
            vmem((tiles, padded, 128), BF16),
            vmem((m - 1, wide, padded, 128), BF16),
            dma((3,)), dma((2,)), dma((2,)), dma((2,)), dma((2,)),
            dma((n - 1,)), dma((n - 1,)), dma((m - 1,)), dma((m - 1,)),
        ],
        compiler_params=pltpu.CompilerParams(
            collective_id=0, has_side_effects=True, vmem_limit_bytes=32 * 1024 * 1024
        ),
    )(*(pltpu.with_memory_space_constraint(x, pltpu.HBM) for x in (volume, weight.T, cotangent)))
    activation, input_grad, weight_grad = pl.pallas_call(
        place,
        out_shape=tuple(jax.ShapeDtypeStruct(r.shape, r.dtype) for r in results),
        in_specs=[pl.BlockSpec(memory_space=pltpu.VMEM)] * 3,
        out_specs=[pl.BlockSpec(memory_space=pl.ANY)] * 3,
        scratch_shapes=[dma((3,))],
    )(*results)
    return activation, input_grad, weight_grad.T


def solution(mesh):
    return jax.shard_map(
        per_device,
        mesh=mesh,
        in_specs=(P("gz", "dp", None, None), P(), P("gz", "dp", None, None)),
        out_specs=(P("gz", "dp", None, None), P("gz", "dp", None, None), P("gz", "dp")),
        check_vma=False,
    )
```

```python
import functools
import math

import jax
import jax.numpy as jnp
from jax import lax
from jax.experimental import pallas as pl
from jax.experimental.pallas import tpu as pltpu
from jax.sharding import PartitionSpec as P

MESH = pl.DeviceIdType.MESH
BF16 = jnp.bfloat16
F32 = jnp.float32


def rolled(x, shift, axis):
    return pltpu.roll(x, shift % x.shape[axis], axis)


def pair_rows(plane, height, pairs):
    return jnp.concatenate([plane[:, 128 * k : 128 * (k + 1)] for k in range(pairs)], axis=0)


def windows(plane, height, pairs):
    own = pair_rows(plane, height, pairs)
    zero = jnp.zeros((height, 128), own.dtype)
    after = jnp.concatenate([own[height:], zero], axis=0)
    before = jnp.concatenate([zero, own[:-height]], axis=0)
    lane = lax.broadcasted_iota(jnp.int32, own.shape, 1)
    return own, jnp.where(lane < 64, after, before)


def y_sum(parts, height):
    row = lax.broadcasted_iota(jnp.int32, (parts.shape[0], 128), 0) % height
    low = jnp.where(row == 0, 0.0, rolled(parts[:, 0:128], 1, 0))
    high = jnp.where(row == height - 1, 0.0, rolled(parts[:, 256:384], -1, 0))
    return parts[:, 128:256] + low + high


def kernel(
    geom, v_ref, w_ref, g_ref, act_ref, ig_ref, wg_ref,
    vbuf, gbuf, wbuf, dbuf, win, dwin, wfwd, wbwd,
    send1, recv1, pack, recv2,
    local_sem, vsend, vrecv, dsend, drecv, ssend1, srecv1, ssend2, srecv2,
):
    n, m, height, pairs, rows_out, cols_out, wide, scale = geom
    me = lax.axis_index("dp")
    my = lax.axis_index("gz")

    barrier = pltpu.get_barrier_semaphore()
    for k in range(1, n):
        pl.semaphore_signal(
            barrier, inc=1, device_id={"dp": lax.rem(me + k, n)}, device_id_type=MESH
        )
    for k in range(1, m):
        pl.semaphore_signal(
            barrier, inc=1, device_id={"gz": lax.rem(my + k, m)}, device_id_type=MESH
        )
    load_w = pltpu.make_async_copy(w_ref, wbuf, local_sem.at[0])
    load_v = pltpu.make_async_copy(v_ref.at[0, 0], vbuf.at[1], local_sem.at[1])
    load_g = pltpu.make_async_copy(g_ref.at[0, 0], gbuf, local_sem.at[2])
    load_w.start()
    load_v.start()
    load_g.start()
    pl.semaphore_wait(barrier, n + m - 2)

    def halo(source, buf, ssem, rsem):
        up = pltpu.make_async_remote_copy(
            src_ref=source, dst_ref=buf.at[0], send_sem=ssem.at[0], recv_sem=rsem.at[0],
            device_id={"dp": lax.rem(me + 1, n)}, device_id_type=MESH,
        )
        down = pltpu.make_async_remote_copy(
            src_ref=source, dst_ref=buf.at[2], send_sem=ssem.at[1], recv_sem=rsem.at[1],
            device_id={"dp": lax.rem(me + n - 1, n)}, device_id_type=MESH,
        )

        @pl.when(me < n - 1)
        def _():
            up.start()

        @pl.when(me > 0)
        def _():
            down.start()

        return up, down

    def halo_arrive(up, down, buf):
        @pl.when(me > 0)
        def _():
            up.wait_recv()

        @pl.when(me == 0)
        def _():
            buf[0] = jnp.zeros(buf.shape[1:], buf.dtype)

        @pl.when(me < n - 1)
        def _():
            down.wait_recv()

        @pl.when(me == n - 1)
        def _():
            buf[2] = jnp.zeros(buf.shape[1:], buf.dtype)

    def halo_sent(up, down):
        @pl.when(me < n - 1)
        def _():
            up.wait_send()

        @pl.when(me > 0)
        def _():
            down.wait_send()

    v_up, v_down = halo(v_ref.at[0, 0], vbuf, vsend, vrecv)

    load_w.wait()
    zero = jnp.zeros((64, 64), BF16)
    for a in range(3):
        for b in range(3):
            base = (a * 9 + b * 3) * 64
            k0, k1, k2 = (wbuf[:, base + 64 * c : base + 64 * (c + 1)] for c in range(3))
            top = jnp.concatenate([k1, k2, zero, k0], axis=1)
            bottom = jnp.concatenate([k0, k1, k2, zero], axis=1)
            wfwd[128 * b : 128 * (b + 1), 256 * a : 256 * (a + 1)] = jnp.concatenate(
                [top, bottom], axis=0
            )
            left = jnp.concatenate([k1, k0, zero, k2], axis=0)
            right = jnp.concatenate([k2, k1, k0, zero], axis=0)
            fa, fb = 2 - a, 2 - b
            wbwd[256 * fa : 256 * (fa + 1), 128 * fb : 128 * (fb + 1)] = jnp.concatenate(
                [left, right], axis=1
            )

    def fill(target, buf, a):
        own, edge = windows(buf[a], height, pairs)
        target[:, 256 * a : 256 * a + 128] = own
        target[:, 256 * a + 128 : 256 * (a + 1)] = edge

    def plane_fwd(a):
        return lax.dot_general(
            win[:, 256 * a : 256 * (a + 1)], wfwd[:, 256 * a : 256 * (a + 1)],
            (((1,), (1,)), ((), ())), preferred_element_type=F32,
        )

    load_v.wait()
    fill(win, vbuf, 1)
    parts = plane_fwd(1)
    load_g.wait()
    halo_arrive(v_up, v_down, vbuf)
    fill(win, vbuf, 0)
    fill(win, vbuf, 2)
    parts = parts + plane_fwd(0) + plane_fwd(2)
    pre = y_sum(parts, height)
    sig = 1.0 / (1.0 + jnp.exp(-pre))
    cot = pair_rows(gbuf[...], height, pairs).astype(F32)
    delta = (cot * sig * (1.0 + pre * (1.0 - sig))).astype(BF16)
    for k in range(pairs):
        dbuf[1, :, 128 * k : 128 * (k + 1)] = delta[height * k : height * (k + 1)]

    wide_delta = delta.astype(F32)
    row = lax.broadcasted_iota(jnp.int32, wide_delta.shape, 0) % height
    ahead = jnp.where(row == height - 1, 0.0, rolled(wide_delta, -1, 0)).astype(BF16)
    behind = jnp.where(row == 0, 0.0, rolled(wide_delta, 1, 0)).astype(BF16)
    moved = jnp.concatenate([ahead, delta, behind], axis=1)
    lane = lax.broadcasted_iota(jnp.int32, (64, 128), 1) < 64
    first_copies = []

    def weight_terms(planes, low_tile, high_tile, stage):
        span = win[:, 256 * planes[0] : 256 * (planes[-1] + 1)]
        terms = lax.dot_general(
            moved, span, (((0,), (0,)), ((), ())), preferred_element_type=F32
        )
        quads = []
        for p in range(len(planes)):
            for b in range(3):
                first = terms[128 * b : 128 * b + 64, 256 * p : 256 * (p + 1)]
                second = terms[128 * b + 64 : 128 * (b + 1), 256 * p : 256 * (p + 1)]
                quads.append((first[:, :128], first[:, 128:], second[:, :128], second[:, 128:]))
        out_tiles = []
        for q in range(0, len(quads), 2):
            a1, a2, b1, b2 = quads[q]
            out_tiles.append(rolled(jnp.where(lane, a1, a2), 64, 1) + b1)
            third = rolled(a1, 64, 1) + b2
            if q + 1 == len(quads):
                out_tiles.append(jnp.where(lane, third, 0.0))
                continue
            c1, c2, e1, e2 = quads[q + 1]
            out_tiles.append(jnp.where(lane, third, c2 + rolled(e1, 64, 1)))
            out_tiles.append(c1 + rolled(jnp.where(lane, e2, e1), 64, 1))
        assert len(out_tiles) == high_tile - low_tile
        for t, tile in enumerate(out_tiles):
            tile = (tile * scale).astype(BF16)
            for d in range(n):
                part = tile[cols_out * d : cols_out * (d + 1)]
                if cols_out % 16:
                    part = jnp.concatenate(
                        [part, jnp.zeros((send1.shape[2] - cols_out, 128), BF16)], axis=0
                    )
                send1[d, low_tile + t] = part
        copies = []
        for k in range(1, n):
            peer = lax.rem(me + k, n)
            copy = pltpu.make_async_remote_copy(
                src_ref=send1.at[peer, low_tile:high_tile],
                dst_ref=recv1.at[k - 1, low_tile:high_tile],
                send_sem=ssend1.at[stage, k - 1], recv_sem=srecv1.at[stage, k - 1],
                device_id={"dp": peer}, device_id_type=MESH,
            )
            copy.start()
            copies.append(copy)
        first_copies.append(copies)

    weight_terms((0, 1), 0, 9, 0)
    weight_terms((2,), 9, 14, 1)

    d_up, d_down = halo(dbuf.at[1], dbuf, dsend, drecv)

    act = (pre * sig).astype(BF16)
    for k in range(pairs):
        act_ref[0, 0, :, 128 * k : 128 * (k + 1)] = act[height * k : height * (k + 1)]

    second_copies = []
    for k in range(1, m):
        peer = lax.rem(my + k, m)
        second_copies.append(pltpu.make_async_remote_copy(
            src_ref=pack.at[peer], dst_ref=recv2.at[k - 1],
            send_sem=ssend2.at[k - 1], recv_sem=srecv2.at[k - 1],
            device_id={"gz": peer}, device_id_type=MESH,
        ))
    early = sum((g + 1) * rows_out <= 9 * 128 for g in range(m))
    summed = []
    lanes = lax.broadcasted_iota(jnp.int32, pack.shape[2:], 1)
    for stage, (low_tile, high_tile) in enumerate(((0, 9), (9, 14))):
        total = send1[me, low_tile:high_tile].astype(F32)
        for k in range(1, n):
            first_copies[stage][k - 1].wait_recv()
            total = total + recv1[k - 1, low_tile:high_tile].astype(F32)
        summed += [total[t] for t in range(high_tile - low_tile)]
        for g in range(early) if stage == 0 else range(early, m):
            start, offset = (g * rows_out) // 128, (g * rows_out) % 128
            for j in range(wide):
                tile = summed[start + j]
                if offset:
                    tile = rolled(tile, -offset, 1)
                    if (g + 1) * rows_out > 128 * (start + j + 1):
                        after = rolled(summed[start + j + 1], -offset, 1)
                        tile = jnp.where(lanes < 128 - offset, tile, after)
                pack[g, j] = tile.astype(BF16)
        for k in range(1, m):
            peer = lax.rem(my + k, m)

            @pl.when((peer < early) if stage == 0 else (peer >= early))
            def _(copy=second_copies[k - 1]):
                copy.start()

    halo_arrive(d_up, d_down, dbuf)
    for a in range(3):
        fill(dwin, dbuf, a)
    back = jnp.dot(dwin[...], wbwd[...], preferred_element_type=F32)
    grad = y_sum(back, height).astype(BF16)
    for k in range(pairs):
        ig_ref[0, 0, :, 128 * k : 128 * (k + 1)] = grad[height * k : height * (k + 1)]

    halo_sent(v_up, v_down)
    halo_sent(d_up, d_down)
    for copy in first_copies[0] + first_copies[1]:
        copy.wait_send()
    total = pack[my].astype(F32)
    for k in range(1, m):
        second_copies[k - 1].wait_recv()
        total = total + recv2[k - 1].astype(F32)
    for t in range(wide):
        count = min(128, rows_out - 128 * t)
        wg_ref[:, 128 * t : 128 * t + count] = total[t, :cols_out, :count]
    for copy in second_copies:
        copy.wait_send()


def place(a_ref, i_ref, w_ref, act_ref, ig_ref, wg_ref, sem):
    pairs = ((a_ref, act_ref), (i_ref, ig_ref), (w_ref, wg_ref))
    copies = [pltpu.make_async_copy(a, b, sem.at[k]) for k, (a, b) in enumerate(pairs)]
    for copy in copies:
        copy.start()
    for copy in copies:
        copy.wait()


def per_device(volume, weight, cotangent):
    n = lax.axis_size("dp")
    m = lax.axis_size("gz")
    chans = weight.shape[1]
    universes, planes, height, merged = volume.shape
    assert chans == 64 and universes == 1 and planes == 1
    pairs = merged // 128
    cells = height * pairs * 2
    rows_out = weight.shape[0] // m
    cols_out = chans // n
    padded = -(-cols_out // 16) * 16
    wide = -(-rows_out // 128)
    tiles = 14
    assert 27 * 64 == weight.shape[0]
    scale = 1.0 / math.sqrt(n * m * cells)
    geom = (n, m, height, pairs, rows_out, cols_out, wide, scale)
    vmem = pltpu.VMEM
    dma = pltpu.SemaphoreType.DMA
    block = (height, merged)
    grid_rows = pairs * height
    results = pl.pallas_call(
        functools.partial(kernel, geom),
        out_shape=(
            vmem(volume.shape, BF16),
            vmem(volume.shape, BF16),
            vmem((cols_out, rows_out), F32),
        ),
        in_specs=[pl.BlockSpec(memory_space=pltpu.HBM)] * 3,
        out_specs=[pl.BlockSpec(memory_space=pltpu.VMEM)] * 3,
        scratch_shapes=[
            vmem((3, *block), BF16),
            vmem(block, BF16),
            vmem(weight.shape[::-1], BF16),
            vmem((3, *block), BF16),
            vmem((grid_rows, 768), BF16),
            vmem((grid_rows, 768), BF16),
            vmem((384, 768), BF16),
            vmem((768, 384), BF16),
            vmem((n, tiles, padded, 128), BF16),
            vmem((n - 1, tiles, padded, 128), BF16),
            vmem((m, wide, padded, 128), BF16),
            vmem((m - 1, wide, padded, 128), BF16),
            dma((3,)), dma((2,)), dma((2,)), dma((2,)), dma((2,)),
            dma((2, n - 1)), dma((2, n - 1)), dma((m - 1,)), dma((m - 1,)),
        ],
        compiler_params=pltpu.CompilerParams(
            collective_id=0, has_side_effects=True, vmem_limit_bytes=32 * 1024 * 1024
        ),
    )(*(pltpu.with_memory_space_constraint(x, pltpu.HBM) for x in (volume, weight.T, cotangent)))
    activation, input_grad, weight_grad = pl.pallas_call(
        place,
        out_shape=tuple(jax.ShapeDtypeStruct(r.shape, r.dtype) for r in results),
        in_specs=[pl.BlockSpec(memory_space=pl.ANY)] * 3,
        out_specs=[pl.BlockSpec(memory_space=pl.ANY)] * 3,
        scratch_shapes=[dma((3,))],
        compiler_params=pltpu.CompilerParams(vmem_limit_bytes=1024 * 1024),
    )(*results)
    return activation, input_grad, weight_grad.T


def solution(mesh):
    return jax.shard_map(
        per_device,
        mesh=mesh,
        in_specs=(P("gz", "dp", None, None), P(), P("gz", "dp", None, None)),
        out_specs=(P("gz", "dp", None, None), P("gz", "dp", None, None), P("gz", "dp")),
        check_vma=False,
    )
```

```python
import functools
import math

import jax
import jax.numpy as jnp
from jax import lax
from jax.experimental import pallas as pl
from jax.experimental.pallas import tpu as pltpu
from jax.sharding import PartitionSpec as P

MESH = pl.DeviceIdType.MESH
BF16 = jnp.bfloat16
F32 = jnp.float32


def rolled(x, shift, axis):
    return pltpu.roll(x, shift % x.shape[axis], axis)


def pair_rows(plane, height, pairs):
    return jnp.concatenate([plane[:, 128 * k : 128 * (k + 1)] for k in range(pairs)], axis=0)


def windows(plane, height, pairs):
    own = pair_rows(plane, height, pairs)
    zero = jnp.zeros((height, 128), own.dtype)
    after = jnp.concatenate([own[height:], zero], axis=0)
    before = jnp.concatenate([zero, own[:-height]], axis=0)
    lane = lax.broadcasted_iota(jnp.int32, own.shape, 1)
    return own, jnp.where(lane < 64, after, before)


def y_sum(parts, height):
    row = lax.broadcasted_iota(jnp.int32, (parts.shape[0], 128), 0) % height
    low = jnp.where(row == 0, 0.0, rolled(parts[:, 0:128], 1, 0))
    high = jnp.where(row == height - 1, 0.0, rolled(parts[:, 256:384], -1, 0))
    return parts[:, 128:256] + low + high


def kernel(
    geom, v_ref, w_ref, g_ref, act_ref, ig_ref, wg_ref,
    vbuf, gbuf, wbuf, dbuf, win, dwin, wfwd, wbwd,
    pack0, recv0, sum0, recv1, sum1, recv2,
    local_sem, vsend, vrecv, dsend, drecv, ssend0, srecv0, ssend1, srecv1, ssend2, srecv2,
):
    n, m, height, pairs, rows_out, cols_out, wide, scale = geom
    me = lax.axis_index("dp")
    my = lax.axis_index("gz")
    mz = m // 2
    z, core = lax.div(my, 2), lax.rem(my, 2)
    partner = my + 1 - 2 * core
    z_peers = [2 * lax.rem(z + k, mz) + core for k in range(1, mz)]

    barrier = pltpu.get_barrier_semaphore()
    for k in range(1, n):
        pl.semaphore_signal(
            barrier, inc=1, device_id={"dp": lax.rem(me + k, n)}, device_id_type=MESH
        )
    for peer in [partner] + z_peers:
        pl.semaphore_signal(barrier, inc=1, device_id={"gz": peer}, device_id_type=MESH)
    load_w = pltpu.make_async_copy(w_ref, wbuf, local_sem.at[0])
    load_v = pltpu.make_async_copy(v_ref.at[0, 0], vbuf.at[1], local_sem.at[1])
    load_g = pltpu.make_async_copy(g_ref.at[0, 0], gbuf, local_sem.at[2])
    load_w.start()
    load_v.start()
    load_g.start()
    pl.semaphore_wait(barrier, n + mz - 1)

    def halo(source, buf, ssem, rsem):
        up = pltpu.make_async_remote_copy(
            src_ref=source, dst_ref=buf.at[0], send_sem=ssem.at[0], recv_sem=rsem.at[0],
            device_id={"dp": lax.rem(me + 1, n)}, device_id_type=MESH,
        )
        down = pltpu.make_async_remote_copy(
            src_ref=source, dst_ref=buf.at[2], send_sem=ssem.at[1], recv_sem=rsem.at[1],
            device_id={"dp": lax.rem(me + n - 1, n)}, device_id_type=MESH,
        )

        @pl.when(me < n - 1)
        def _():
            up.start()

        @pl.when(me > 0)
        def _():
            down.start()

        return up, down

    def halo_arrive(up, down, buf):
        @pl.when(me > 0)
        def _():
            up.wait_recv()

        @pl.when(me == 0)
        def _():
            buf[0] = jnp.zeros(buf.shape[1:], buf.dtype)

        @pl.when(me < n - 1)
        def _():
            down.wait_recv()

        @pl.when(me == n - 1)
        def _():
            buf[2] = jnp.zeros(buf.shape[1:], buf.dtype)

    def halo_sent(up, down):
        @pl.when(me < n - 1)
        def _():
            up.wait_send()

        @pl.when(me > 0)
        def _():
            down.wait_send()

    v_up, v_down = halo(v_ref.at[0, 0], vbuf, vsend, vrecv)

    load_w.wait()
    zero = jnp.zeros((64, 64), BF16)
    for a in range(3):
        for b in range(3):
            base = (a * 9 + b * 3) * 64
            k0, k1, k2 = (wbuf[:, base + 64 * c : base + 64 * (c + 1)] for c in range(3))
            top = jnp.concatenate([k1, k2, zero, k0], axis=1)
            bottom = jnp.concatenate([k0, k1, k2, zero], axis=1)
            wfwd[128 * b : 128 * (b + 1), 256 * a : 256 * (a + 1)] = jnp.concatenate(
                [top, bottom], axis=0
            )
            left = jnp.concatenate([k1, k0, zero, k2], axis=0)
            right = jnp.concatenate([k2, k1, k0, zero], axis=0)
            fa, fb = 2 - a, 2 - b
            wbwd[256 * fa : 256 * (fa + 1), 128 * fb : 128 * (fb + 1)] = jnp.concatenate(
                [left, right], axis=1
            )

    def fill(target, buf, a):
        own, edge = windows(buf[a], height, pairs)
        target[:, 256 * a : 256 * a + 128] = own
        target[:, 256 * a + 128 : 256 * (a + 1)] = edge

    def plane_fwd(a):
        return lax.dot_general(
            win[:, 256 * a : 256 * (a + 1)], wfwd[:, 256 * a : 256 * (a + 1)],
            (((1,), (1,)), ((), ())), preferred_element_type=F32,
        )

    load_v.wait()
    fill(win, vbuf, 1)
    parts = plane_fwd(1)
    load_g.wait()
    halo_arrive(v_up, v_down, vbuf)
    fill(win, vbuf, 0)
    fill(win, vbuf, 2)
    parts = parts + plane_fwd(0) + plane_fwd(2)
    pre = y_sum(parts, height)
    sig = 1.0 / (1.0 + jnp.exp(-pre))
    cot = pair_rows(gbuf[...], height, pairs).astype(F32)
    delta = (cot * sig * (1.0 + pre * (1.0 - sig))).astype(BF16)
    for k in range(pairs):
        dbuf[1, :, 128 * k : 128 * (k + 1)] = delta[height * k : height * (k + 1)]

    d_up, d_down = halo(dbuf.at[1], dbuf, dsend, drecv)

    wide_delta = delta.astype(F32)
    row = lax.broadcasted_iota(jnp.int32, wide_delta.shape, 0) % height
    ahead = jnp.where(row == height - 1, 0.0, rolled(wide_delta, -1, 0)).astype(BF16)
    behind = jnp.where(row == 0, 0.0, rolled(wide_delta, 1, 0)).astype(BF16)
    moved = jnp.concatenate([ahead, delta, behind], axis=1)
    lane = lax.broadcasted_iota(jnp.int32, (64, 128), 1) < 64
    early = sum(2 * (q + 1) * rows_out <= 9 * 128 for q in range(mz))
    parts_z = ((0, early), (early, mz))
    zero_copies = []
    gathered = []
    lanes = lax.broadcasted_iota(jnp.int32, (64, 128), 1)

    def weight_terms(planes, low_z, high_z, stage):
        span = win[:, 256 * planes[0] : 256 * (planes[-1] + 1)]
        terms = lax.dot_general(
            moved, span, (((0,), (0,)), ((), ())), preferred_element_type=F32
        )
        quads = []
        for p in range(len(planes)):
            for b in range(3):
                first = terms[128 * b : 128 * b + 64, 256 * p : 256 * (p + 1)]
                second = terms[128 * b + 64 : 128 * (b + 1), 256 * p : 256 * (p + 1)]
                quads.append((first[:, :128], first[:, 128:], second[:, :128], second[:, 128:]))
        out_tiles = []
        for q in range(0, len(quads), 2):
            a1, a2, b1, b2 = quads[q]
            out_tiles.append(rolled(jnp.where(lane, a1, a2), 64, 1) + b1)
            third = rolled(a1, 64, 1) + b2
            if q + 1 == len(quads):
                out_tiles.append(jnp.where(lane, third, 0.0))
                continue
            c1, c2, e1, e2 = quads[q + 1]
            out_tiles.append(jnp.where(lane, third, c2 + rolled(e1, 64, 1)))
            out_tiles.append(c1 + rolled(jnp.where(lane, e2, e1), 64, 1))
        gathered.extend(tile * scale for tile in out_tiles)
        for g in range(2 * low_z, 2 * high_z):
            start, offset = (g * rows_out) // 128, (g * rows_out) % 128
            for j in range(wide):
                tile = gathered[start + j]
                if offset:
                    tile = rolled(tile, -offset, 1)
                    if (g + 1) * rows_out > 128 * (start + j + 1):
                        after = rolled(gathered[start + j + 1], -offset, 1)
                        tile = jnp.where(lanes < 128 - offset, tile, after)
                tile = tile.astype(BF16)
                for d in range(n):
                    part = tile[cols_out * d : cols_out * (d + 1)]
                    if cols_out % 16:
                        fill_rows = jnp.zeros((pack0.shape[4] - cols_out, 128), BF16)
                        part = jnp.concatenate([part, fill_rows], axis=0)
                    pack0[g % 2, g // 2, d, j] = part
        copy = pltpu.make_async_remote_copy(
            src_ref=pack0.at[1 - core, low_z:high_z], dst_ref=recv0.at[low_z:high_z],
            send_sem=ssend0.at[stage], recv_sem=srecv0.at[stage],
            device_id={"gz": partner}, device_id_type=MESH,
        )
        copy.start()
        zero_copies.append(copy)

    weight_terms((0, 1), 0, early, 0)
    weight_terms((2,), early, mz, 1)

    act = (pre * sig).astype(BF16)
    for k in range(pairs):
        act_ref[0, 0, :, 128 * k : 128 * (k + 1)] = act[height * k : height * (k + 1)]

    first_copies = []
    for stage, (low_z, high_z) in enumerate(parts_z):
        zero_copies[stage].wait_recv()
        both = pack0[core, low_z:high_z].astype(F32) + recv0[low_z:high_z].astype(F32)
        sum0[low_z:high_z] = both.astype(BF16)
        copies = []
        for k in range(1, n):
            peer = lax.rem(me + k, n)
            copy = pltpu.make_async_remote_copy(
                src_ref=sum0.at[low_z:high_z, peer], dst_ref=recv1.at[k - 1, low_z:high_z],
                send_sem=ssend1.at[stage, k - 1], recv_sem=srecv1.at[stage, k - 1],
                device_id={"dp": peer}, device_id_type=MESH,
            )
            copy.start()
            copies.append(copy)
        first_copies.append(copies)

    halo_arrive(d_up, d_down, dbuf)
    for a in range(3):
        fill(dwin, dbuf, a)
    back = jnp.dot(dwin[...], wbwd[...], preferred_element_type=F32)
    grad = y_sum(back, height).astype(BF16)
    for k in range(pairs):
        ig_ref[0, 0, :, 128 * k : 128 * (k + 1)] = grad[height * k : height * (k + 1)]

    second_copies = []
    for k in range(1, mz):
        second_copies.append(pltpu.make_async_remote_copy(
            src_ref=sum1.at[lax.rem(z + k, mz)], dst_ref=recv2.at[k - 1],
            send_sem=ssend2.at[k - 1], recv_sem=srecv2.at[k - 1],
            device_id={"gz": z_peers[k - 1]}, device_id_type=MESH,
        ))
    for stage, (low_z, high_z) in enumerate(parts_z):
        total = sum0[low_z:high_z, me].astype(F32)
        for k in range(1, n):
            first_copies[stage][k - 1].wait_recv()
            total = total + recv1[k - 1, low_z:high_z].astype(F32)
        sum1[low_z:high_z] = total.astype(BF16)
        for k in range(1, mz):
            target = lax.rem(z + k, mz)

            @pl.when((target < early) if stage == 0 else (target >= early))
            def _(copy=second_copies[k - 1]):
                copy.start()

    halo_sent(v_up, v_down)
    halo_sent(d_up, d_down)
    for copy in zero_copies + first_copies[0] + first_copies[1]:
        copy.wait_send()
    total = sum1[z].astype(F32)
    for k in range(1, mz):
        second_copies[k - 1].wait_recv()
        total = total + recv2[k - 1].astype(F32)
    for t in range(wide):
        count = min(128, rows_out - 128 * t)
        wg_ref[:, 128 * t : 128 * t + count] = total[t, :cols_out, :count]
    for copy in second_copies:
        copy.wait_send()


def place(a_ref, i_ref, w_ref, act_ref, ig_ref, wg_ref, sem):
    pairs = ((a_ref, act_ref), (i_ref, ig_ref), (w_ref, wg_ref))
    copies = [pltpu.make_async_copy(a, b, sem.at[k]) for k, (a, b) in enumerate(pairs)]
    for copy in copies:
        copy.start()
    for copy in copies:
        copy.wait()


def per_device(volume, weight, cotangent):
    n = lax.axis_size("dp")
    m = lax.axis_size("gz")
    chans = weight.shape[1]
    universes, planes, height, merged = volume.shape
    assert chans == 64 and universes == 1 and planes == 1
    pairs = merged // 128
    cells = height * pairs * 2
    rows_out = weight.shape[0] // m
    cols_out = chans // n
    padded = -(-cols_out // 16) * 16
    wide = -(-rows_out // 128)
    assert 27 * 64 == weight.shape[0]
    scale = 1.0 / math.sqrt(n * m * cells)
    geom = (n, m, height, pairs, rows_out, cols_out, wide, scale)
    vmem = pltpu.VMEM
    dma = pltpu.SemaphoreType.DMA
    block = (height, merged)
    grid_rows = pairs * height
    results = pl.pallas_call(
        functools.partial(kernel, geom),
        out_shape=(
            vmem(volume.shape, BF16),
            vmem(volume.shape, BF16),
            vmem((cols_out, rows_out), F32),
        ),
        in_specs=[pl.BlockSpec(memory_space=pltpu.HBM)] * 3,
        out_specs=[pl.BlockSpec(memory_space=pltpu.VMEM)] * 3,
        scratch_shapes=[
            vmem((3, *block), BF16),
            vmem(block, BF16),
            vmem(weight.shape[::-1], BF16),
            vmem((3, *block), BF16),
            vmem((grid_rows, 768), BF16),
            vmem((grid_rows, 768), BF16),
            vmem((384, 768), BF16),
            vmem((768, 384), BF16),
            vmem((2, m // 2, n, wide, padded, 128), BF16),
            vmem((m // 2, n, wide, padded, 128), BF16),
            vmem((m // 2, n, wide, padded, 128), BF16),
            vmem((n - 1, m // 2, wide, padded, 128), BF16),
            vmem((m // 2, wide, padded, 128), BF16),
            vmem((m // 2 - 1, wide, padded, 128), BF16),
            dma((3,)), dma((2,)), dma((2,)), dma((2,)), dma((2,)),
            dma((2,)), dma((2,)), dma((2, n - 1)), dma((2, n - 1)),
            dma((m // 2 - 1,)), dma((m // 2 - 1,)),
        ],
        compiler_params=pltpu.CompilerParams(
            collective_id=0, has_side_effects=True, vmem_limit_bytes=32 * 1024 * 1024
        ),
    )(*(pltpu.with_memory_space_constraint(x, pltpu.HBM) for x in (volume, weight.T, cotangent)))
    activation, input_grad, weight_grad = pl.pallas_call(
        place,
        out_shape=tuple(jax.ShapeDtypeStruct(r.shape, r.dtype) for r in results),
        in_specs=[pl.BlockSpec(memory_space=pl.ANY)] * 3,
        out_specs=[pl.BlockSpec(memory_space=pl.ANY)] * 3,
        scratch_shapes=[dma((3,))],
        compiler_params=pltpu.CompilerParams(vmem_limit_bytes=1024 * 1024),
    )(*results)
    return activation, input_grad, weight_grad.T


def solution(mesh):
    return jax.shard_map(
        per_device,
        mesh=mesh,
        in_specs=(P("gz", "dp", None, None), P(), P("gz", "dp", None, None)),
        out_specs=(P("gz", "dp", None, None), P("gz", "dp", None, None), P("gz", "dp")),
        check_vma=False,
    )
```

```python
import functools
import math

import jax
import jax.numpy as jnp
from jax import lax
from jax.experimental import pallas as pl
from jax.experimental.pallas import tpu as pltpu
from jax.sharding import PartitionSpec as P

MESH = pl.DeviceIdType.MESH
BF16 = jnp.bfloat16
F32 = jnp.float32


def rolled(x, shift, axis):
    return pltpu.roll(x, shift % x.shape[axis], axis)


def pair_rows(plane, height, pairs):
    return jnp.concatenate([plane[:, 128 * k : 128 * (k + 1)] for k in range(pairs)], axis=0)


def windows(plane, height, pairs):
    own = pair_rows(plane, height, pairs)
    zero = jnp.zeros((height, 128), own.dtype)
    after = jnp.concatenate([own[height:], zero], axis=0)
    before = jnp.concatenate([zero, own[:-height]], axis=0)
    lane = lax.broadcasted_iota(jnp.int32, own.shape, 1)
    return own, jnp.where(lane < 64, after, before)


def y_sum(parts, height):
    row = lax.broadcasted_iota(jnp.int32, (parts.shape[0], 128), 0) % height
    low = jnp.where(row == 0, 0.0, rolled(parts[:, 0:128], 1, 0))
    high = jnp.where(row == height - 1, 0.0, rolled(parts[:, 256:384], -1, 0))
    return parts[:, 128:256] + low + high


def kernel(
    geom, v_ref, w_ref, g_ref, act_ref, ig_ref, wg_ref,
    vbuf, gbuf, wbuf, dbuf, win, dwin, wfwd, wbwd,
    pack0, recv0, sum0, recv1, sum1, recv2,
    local_sem, vsend, vrecv, dsend, drecv, ssend0, srecv0, ssend1, srecv1, ssend2, srecv2,
):
    n, m, height, pairs, rows_out, cols_out, wide, scale = geom
    me = lax.axis_index("dp")
    my = lax.axis_index("gz")
    mz = m // 2
    z, core = lax.div(my, 2), lax.rem(my, 2)
    partner = my + 1 - 2 * core
    z_peers = [2 * lax.rem(z + k, mz) + core for k in range(1, mz)]

    barrier = pltpu.get_barrier_semaphore()
    for k in range(1, n):
        pl.semaphore_signal(
            barrier, inc=1, device_id={"dp": lax.rem(me + k, n)}, device_id_type=MESH
        )
    for peer in [partner] + z_peers:
        pl.semaphore_signal(barrier, inc=1, device_id={"gz": peer}, device_id_type=MESH)
    load_w = pltpu.make_async_copy(w_ref, wbuf, local_sem.at[0])
    load_v = pltpu.make_async_copy(v_ref.at[0, 0], vbuf.at[1], local_sem.at[1])
    load_g = pltpu.make_async_copy(g_ref.at[0, 0], gbuf, local_sem.at[2])
    load_w.start()
    load_v.start()
    load_g.start()
    pl.semaphore_wait(barrier, n + mz - 1)

    def halo(source, buf, ssem, rsem):
        up = pltpu.make_async_remote_copy(
            src_ref=source, dst_ref=buf.at[0], send_sem=ssem.at[0], recv_sem=rsem.at[0],
            device_id={"dp": lax.rem(me + 1, n)}, device_id_type=MESH,
        )
        down = pltpu.make_async_remote_copy(
            src_ref=source, dst_ref=buf.at[2], send_sem=ssem.at[1], recv_sem=rsem.at[1],
            device_id={"dp": lax.rem(me + n - 1, n)}, device_id_type=MESH,
        )

        @pl.when(me < n - 1)
        def _():
            up.start()

        @pl.when(me > 0)
        def _():
            down.start()

        return up, down

    def arrive_low(up, buf):
        @pl.when(me > 0)
        def _():
            up.wait_recv()

        @pl.when(me == 0)
        def _():
            buf[0] = jnp.zeros(buf.shape[1:], buf.dtype)

    def arrive_high(down, buf):
        @pl.when(me < n - 1)
        def _():
            down.wait_recv()

        @pl.when(me == n - 1)
        def _():
            buf[2] = jnp.zeros(buf.shape[1:], buf.dtype)

    lower = me < n // 2
    near = jnp.where(lower, 0, 2)

    def halo_near(up, down, buf):
        @pl.when(lower)
        def _():
            arrive_low(up, buf)

        @pl.when(jnp.logical_not(lower))
        def _():
            arrive_high(down, buf)

    def halo_far(up, down, buf):
        @pl.when(lower)
        def _():
            arrive_high(down, buf)

        @pl.when(jnp.logical_not(lower))
        def _():
            arrive_low(up, buf)

    def halo_sent(up, down):
        @pl.when(me < n - 1)
        def _():
            up.wait_send()

        @pl.when(me > 0)
        def _():
            down.wait_send()

    v_up, v_down = halo(v_ref.at[0, 0], vbuf, vsend, vrecv)

    load_w.wait()
    zero = jnp.zeros((64, 64), BF16)
    for a in range(3):
        for b in range(3):
            base = (a * 9 + b * 3) * 64
            k0, k1, k2 = (wbuf[:, base + 64 * c : base + 64 * (c + 1)] for c in range(3))
            top = jnp.concatenate([k1, k2, zero, k0], axis=1)
            bottom = jnp.concatenate([k0, k1, k2, zero], axis=1)
            wfwd[128 * b : 128 * (b + 1), 256 * a : 256 * (a + 1)] = jnp.concatenate(
                [top, bottom], axis=0
            )
            left = jnp.concatenate([k1, k0, zero, k2], axis=0)
            right = jnp.concatenate([k2, k1, k0, zero], axis=0)
            fa, fb = 2 - a, 2 - b
            wbwd[256 * fa : 256 * (fa + 1), 128 * fb : 128 * (fb + 1)] = jnp.concatenate(
                [left, right], axis=1
            )

    def fill(target, buf, a):
        own, edge = windows(buf[a], height, pairs)
        start = a * 256 if isinstance(a, int) else pl.multiple_of(a * 256, 256)
        target[:, pl.ds(start, 256)] = jnp.concatenate([own, edge], axis=1)

    def plane_fwd(a):
        start = a * 256 if isinstance(a, int) else pl.multiple_of(a * 256, 256)
        return lax.dot_general(
            win[:, pl.ds(start, 256)], wfwd[:, pl.ds(start, 256)],
            (((1,), (1,)), ((), ())), preferred_element_type=F32,
        )

    def plane_bwd(a):
        start = a * 256 if isinstance(a, int) else pl.multiple_of(a * 256, 256)
        return jnp.dot(
            dwin[:, pl.ds(start, 256)], wbwd[pl.ds(start, 256), :], preferred_element_type=F32
        )

    load_v.wait()
    fill(win, vbuf, 1)
    parts = plane_fwd(1)
    load_g.wait()
    halo_near(v_up, v_down, vbuf)
    fill(win, vbuf, near)
    parts = parts + plane_fwd(near)
    halo_far(v_up, v_down, vbuf)
    fill(win, vbuf, 2 - near)
    parts = parts + plane_fwd(2 - near)
    pre = y_sum(parts, height)
    sig = 1.0 / (1.0 + jnp.exp(-pre))
    cot = pair_rows(gbuf[...], height, pairs).astype(F32)
    delta = (cot * sig * (1.0 + pre * (1.0 - sig))).astype(BF16)
    for k in range(pairs):
        dbuf[1, :, 128 * k : 128 * (k + 1)] = delta[height * k : height * (k + 1)]

    d_up, d_down = halo(dbuf.at[1], dbuf, dsend, drecv)

    wide_delta = delta.astype(F32)
    row = lax.broadcasted_iota(jnp.int32, wide_delta.shape, 0) % height
    ahead = jnp.where(row == height - 1, 0.0, rolled(wide_delta, -1, 0)).astype(BF16)
    behind = jnp.where(row == 0, 0.0, rolled(wide_delta, 1, 0)).astype(BF16)
    moved = jnp.concatenate([ahead, delta, behind], axis=1)
    lane = lax.broadcasted_iota(jnp.int32, (64, 128), 1) < 64
    early = sum(2 * (q + 1) * rows_out <= 9 * 128 for q in range(mz))
    parts_z = ((0, early), (early, mz))
    zero_copies = []
    gathered = []
    lanes = lax.broadcasted_iota(jnp.int32, (64, 128), 1)

    def weight_terms(planes, low_z, high_z, stage):
        span = win[:, 256 * planes[0] : 256 * (planes[-1] + 1)]
        terms = lax.dot_general(
            moved, span, (((0,), (0,)), ((), ())), preferred_element_type=F32
        )
        quads = []
        for p in range(len(planes)):
            for b in range(3):
                first = terms[128 * b : 128 * b + 64, 256 * p : 256 * (p + 1)]
                second = terms[128 * b + 64 : 128 * (b + 1), 256 * p : 256 * (p + 1)]
                quads.append((first[:, :128], first[:, 128:], second[:, :128], second[:, 128:]))
        out_tiles = []
        for q in range(0, len(quads), 2):
            a1, a2, b1, b2 = quads[q]
            out_tiles.append(rolled(jnp.where(lane, a1, a2), 64, 1) + b1)
            third = rolled(a1, 64, 1) + b2
            if q + 1 == len(quads):
                out_tiles.append(jnp.where(lane, third, 0.0))
                continue
            c1, c2, e1, e2 = quads[q + 1]
            out_tiles.append(jnp.where(lane, third, c2 + rolled(e1, 64, 1)))
            out_tiles.append(c1 + rolled(jnp.where(lane, e2, e1), 64, 1))
        gathered.extend(tile * scale for tile in out_tiles)
        for g in range(2 * low_z, 2 * high_z):
            start, offset = (g * rows_out) // 128, (g * rows_out) % 128
            for j in range(wide):
                tile = gathered[start + j]
                if offset:
                    tile = rolled(tile, -offset, 1)
                    if (g + 1) * rows_out > 128 * (start + j + 1):
                        after = rolled(gathered[start + j + 1], -offset, 1)
                        tile = jnp.where(lanes < 128 - offset, tile, after)
                tile = tile.astype(BF16)
                for d in range(n):
                    part = tile[cols_out * d : cols_out * (d + 1)]
                    if cols_out % 16:
                        fill_rows = jnp.zeros((pack0.shape[4] - cols_out, 128), BF16)
                        part = jnp.concatenate([part, fill_rows], axis=0)
                    pack0[g % 2, g // 2, d, j] = part
        copy = pltpu.make_async_remote_copy(
            src_ref=pack0.at[1 - core, low_z:high_z], dst_ref=recv0.at[low_z:high_z],
            send_sem=ssend0.at[stage], recv_sem=srecv0.at[stage],
            device_id={"gz": partner}, device_id_type=MESH,
        )
        copy.start()
        zero_copies.append(copy)

    weight_terms((0, 1), 0, early, 0)
    weight_terms((2,), early, mz, 1)

    act = (pre * sig).astype(BF16)
    for k in range(pairs):
        act_ref[0, 0, :, 128 * k : 128 * (k + 1)] = act[height * k : height * (k + 1)]

    first_copies = []
    for stage, (low_z, high_z) in enumerate(parts_z):
        zero_copies[stage].wait_recv()
        both = pack0[core, low_z:high_z].astype(F32) + recv0[low_z:high_z].astype(F32)
        sum0[low_z:high_z] = both.astype(BF16)
        copies = []
        for k in range(1, n):
            peer = lax.rem(me + k, n)
            copy = pltpu.make_async_remote_copy(
                src_ref=sum0.at[low_z:high_z, peer], dst_ref=recv1.at[k - 1, low_z:high_z],
                send_sem=ssend1.at[stage, k - 1], recv_sem=srecv1.at[stage, k - 1],
                device_id={"dp": peer}, device_id_type=MESH,
            )
            copy.start()
            copies.append(copy)
        first_copies.append(copies)

    second_copies = []
    for k in range(1, mz):
        second_copies.append(pltpu.make_async_remote_copy(
            src_ref=sum1.at[lax.rem(z + k, mz)], dst_ref=recv2.at[k - 1],
            send_sem=ssend2.at[k - 1], recv_sem=srecv2.at[k - 1],
            device_id={"gz": z_peers[k - 1]}, device_id_type=MESH,
        ))
    for stage, (low_z, high_z) in enumerate(parts_z):
        total = sum0[low_z:high_z, me].astype(F32)
        for k in range(1, n):
            first_copies[stage][k - 1].wait_recv()
            total = total + recv1[k - 1, low_z:high_z].astype(F32)
        sum1[low_z:high_z] = total.astype(BF16)
        for k in range(1, mz):
            target = lax.rem(z + k, mz)

            @pl.when((target < early) if stage == 0 else (target >= early))
            def _(copy=second_copies[k - 1]):
                copy.start()

    fill(dwin, dbuf, 1)
    back = plane_bwd(1)
    halo_near(d_up, d_down, dbuf)
    fill(dwin, dbuf, near)
    back = back + plane_bwd(near)
    halo_far(d_up, d_down, dbuf)
    fill(dwin, dbuf, 2 - near)
    back = back + plane_bwd(2 - near)
    grad = y_sum(back, height).astype(BF16)
    for k in range(pairs):
        ig_ref[0, 0, :, 128 * k : 128 * (k + 1)] = grad[height * k : height * (k + 1)]

    halo_sent(v_up, v_down)
    halo_sent(d_up, d_down)
    for copy in zero_copies + first_copies[0] + first_copies[1]:
        copy.wait_send()
    total = sum1[z].astype(F32)
    for k in range(1, mz):
        second_copies[k - 1].wait_recv()
        total = total + recv2[k - 1].astype(F32)
    for t in range(wide):
        count = min(128, rows_out - 128 * t)
        wg_ref[:, 128 * t : 128 * t + count] = total[t, :cols_out, :count]
    for copy in second_copies:
        copy.wait_send()


def place(a_ref, i_ref, w_ref, act_ref, ig_ref, wg_ref, sem):
    pairs = ((a_ref, act_ref), (i_ref, ig_ref), (w_ref, wg_ref))
    copies = [pltpu.make_async_copy(a, b, sem.at[k]) for k, (a, b) in enumerate(pairs)]
    for copy in copies:
        copy.start()
    for copy in copies:
        copy.wait()


def per_device(volume, weight, cotangent):
    n = lax.axis_size("dp")
    m = lax.axis_size("gz")
    chans = weight.shape[1]
    universes, planes, height, merged = volume.shape
    assert chans == 64 and universes == 1 and planes == 1
    pairs = merged // 128
    cells = height * pairs * 2
    rows_out = weight.shape[0] // m
    cols_out = chans // n
    padded = -(-cols_out // 16) * 16
    wide = -(-rows_out // 128)
    assert 27 * 64 == weight.shape[0]
    scale = 1.0 / math.sqrt(n * m * cells)
    geom = (n, m, height, pairs, rows_out, cols_out, wide, scale)
    vmem = pltpu.VMEM
    dma = pltpu.SemaphoreType.DMA
    block = (height, merged)
    grid_rows = pairs * height
    results = pl.pallas_call(
        functools.partial(kernel, geom),
        out_shape=(
            vmem(volume.shape, BF16),
            vmem(volume.shape, BF16),
            vmem((cols_out, rows_out), F32),
        ),
        in_specs=[pl.BlockSpec(memory_space=pltpu.HBM)] * 3,
        out_specs=[pl.BlockSpec(memory_space=pltpu.VMEM)] * 3,
        scratch_shapes=[
            vmem((3, *block), BF16),
            vmem(block, BF16),
            vmem(weight.shape[::-1], BF16),
            vmem((3, *block), BF16),
            vmem((grid_rows, 768), BF16),
            vmem((grid_rows, 768), BF16),
            vmem((384, 768), BF16),
            vmem((768, 384), BF16),
            vmem((2, m // 2, n, wide, padded, 128), BF16),
            vmem((m // 2, n, wide, padded, 128), BF16),
            vmem((m // 2, n, wide, padded, 128), BF16),
            vmem((n - 1, m // 2, wide, padded, 128), BF16),
            vmem((m // 2, wide, padded, 128), BF16),
            vmem((m // 2 - 1, wide, padded, 128), BF16),
            dma((3,)), dma((2,)), dma((2,)), dma((2,)), dma((2,)),
            dma((2,)), dma((2,)), dma((2, n - 1)), dma((2, n - 1)),
            dma((m // 2 - 1,)), dma((m // 2 - 1,)),
        ],
        compiler_params=pltpu.CompilerParams(
            collective_id=0, has_side_effects=True, vmem_limit_bytes=32 * 1024 * 1024
        ),
    )(*(pltpu.with_memory_space_constraint(x, pltpu.HBM) for x in (volume, weight.T, cotangent)))
    activation, input_grad, weight_grad = pl.pallas_call(
        place,
        out_shape=tuple(jax.ShapeDtypeStruct(r.shape, r.dtype) for r in results),
        in_specs=[pl.BlockSpec(memory_space=pl.ANY)] * 3,
        out_specs=[pl.BlockSpec(memory_space=pl.ANY)] * 3,
        scratch_shapes=[dma((3,))],
        compiler_params=pltpu.CompilerParams(vmem_limit_bytes=1024 * 1024),
    )(*results)
    return activation, input_grad, weight_grad.T


def solution(mesh):
    return jax.shard_map(
        per_device,
        mesh=mesh,
        in_specs=(P("gz", "dp", None, None), P(), P("gz", "dp", None, None)),
        out_specs=(P("gz", "dp", None, None), P("gz", "dp", None, None), P("gz", "dp")),
        check_vma=False,
    )
```

```python
import functools
import math

import jax
import jax.numpy as jnp
from jax import lax
from jax.experimental import pallas as pl
from jax.experimental.pallas import tpu as pltpu
from jax.sharding import PartitionSpec as P

MESH = pl.DeviceIdType.MESH
BF16 = jnp.bfloat16
F32 = jnp.float32


def rolled(x, shift, axis):
    return pltpu.roll(x, shift % x.shape[axis], axis)


def pair_rows(plane, height, pairs):
    return jnp.concatenate([plane[:, 128 * k : 128 * (k + 1)] for k in range(pairs)], axis=0)


def windows(buf, a, height, low, high):
    zero = jnp.zeros((height, 128), buf.dtype)
    count = buf.shape[2] // 128

    def column(k):
        return buf[a, :, 128 * k : 128 * (k + 1)] if 0 <= k < count else zero

    own, after, before = (
        jnp.concatenate([column(k + shift) for k in range(low, high)], axis=0)
        for shift in (0, 1, -1)
    )
    lane = lax.broadcasted_iota(jnp.int32, own.shape, 1)
    return own, jnp.where(lane < 64, after, before)


def y_sum(parts, height):
    row = lax.broadcasted_iota(jnp.int32, (parts.shape[0], 128), 0) % height
    low = jnp.where(row == 0, 0.0, rolled(parts[:, 0:128], 1, 0))
    high = jnp.where(row == height - 1, 0.0, rolled(parts[:, 256:384], -1, 0))
    return parts[:, 128:256] + low + high


def kernel(
    geom, v_ref, w_ref, g_ref, act_ref, ig_ref, wg_ref,
    vbuf, gbuf, wbuf, dbuf, win, dwin, wfwd, wbwd,
    pack0, recv0, sum0, recv1, sum1, recv2,
    local_sem, vsend, vrecv, dsend, drecv, ssend0, srecv0, ssend1, srecv1, ssend2, srecv2,
):
    n, m, height, pairs, rows_out, cols_out, wide, scale = geom
    me = lax.axis_index("dp")
    my = lax.axis_index("gz")
    mz = m // 2
    z, core = lax.div(my, 2), lax.rem(my, 2)
    partner = my + 1 - 2 * core
    z_peers = [2 * lax.rem(z + k, mz) + core for k in range(1, mz)]

    barrier = pltpu.get_barrier_semaphore()
    for k in range(1, n):
        pl.semaphore_signal(
            barrier, inc=1, device_id={"dp": lax.rem(me + k, n)}, device_id_type=MESH
        )
    for peer in [partner] + z_peers:
        pl.semaphore_signal(barrier, inc=1, device_id={"gz": peer}, device_id_type=MESH)
    load_w = pltpu.make_async_copy(w_ref, wbuf, local_sem.at[0])
    load_v = pltpu.make_async_copy(v_ref.at[0, 0], vbuf.at[1], local_sem.at[1])
    load_g = pltpu.make_async_copy(g_ref.at[0, 0], gbuf, local_sem.at[2])
    load_w.start()
    load_v.start()
    load_g.start()
    pl.semaphore_wait(barrier, n + mz - 1)

    def halo(source, buf, ssem, rsem, piece, low, high):
        up = pltpu.make_async_remote_copy(
            src_ref=source.at[:, low:high], dst_ref=buf.at[0, :, low:high],
            send_sem=ssem.at[piece, 0], recv_sem=rsem.at[piece, 0],
            device_id={"dp": lax.rem(me + 1, n)}, device_id_type=MESH,
        )
        down = pltpu.make_async_remote_copy(
            src_ref=source.at[:, low:high], dst_ref=buf.at[2, :, low:high],
            send_sem=ssem.at[piece, 1], recv_sem=rsem.at[piece, 1],
            device_id={"dp": lax.rem(me + n - 1, n)}, device_id_type=MESH,
        )

        @pl.when(me < n - 1)
        def _():
            up.start()

        @pl.when(me > 0)
        def _():
            down.start()

        return up, down, buf, low, high

    def halo_arrive(up, down, buf, low, high):
        @pl.when(me > 0)
        def _():
            up.wait_recv()

        @pl.when(me == 0)
        def _():
            buf[0, :, low:high] = jnp.zeros((height, high - low), buf.dtype)

        @pl.when(me < n - 1)
        def _():
            down.wait_recv()

        @pl.when(me == n - 1)
        def _():
            buf[2, :, low:high] = jnp.zeros((height, high - low), buf.dtype)

    def halo_sent(up, down, *_):
        @pl.when(me < n - 1)
        def _():
            up.wait_send()

        @pl.when(me > 0)
        def _():
            down.wait_send()

    half = pairs // 2
    cut = 128 * (half + 1)
    v_halos = [
        halo(v_ref.at[0, 0], vbuf, vsend, vrecv, piece, low, high)
        for piece, (low, high) in enumerate(((0, cut), (cut, 128 * pairs)))
    ]

    load_w.wait()
    zero = jnp.zeros((64, 64), BF16)
    for a in range(3):
        for b in range(3):
            base = (a * 9 + b * 3) * 64
            k0, k1, k2 = (wbuf[:, base + 64 * c : base + 64 * (c + 1)] for c in range(3))
            top = jnp.concatenate([k1, k2, zero, k0], axis=1)
            bottom = jnp.concatenate([k0, k1, k2, zero], axis=1)
            wfwd[128 * b : 128 * (b + 1), 256 * a : 256 * (a + 1)] = jnp.concatenate(
                [top, bottom], axis=0
            )
            left = jnp.concatenate([k1, k0, zero, k2], axis=0)
            right = jnp.concatenate([k2, k1, k0, zero], axis=0)
            fa, fb = 2 - a, 2 - b
            wbwd[256 * fa : 256 * (fa + 1), 128 * fb : 128 * (fb + 1)] = jnp.concatenate(
                [left, right], axis=1
            )

    def fill(target, buf, a, low, high):
        own, edge = windows(buf, a, height, low, high)
        target[height * low : height * high, 256 * a : 256 * a + 128] = own
        target[height * low : height * high, 256 * a + 128 : 256 * (a + 1)] = edge

    def plane_fwd(a, rows):
        return lax.dot_general(
            win[rows, 256 * a : 256 * (a + 1)], wfwd[:, 256 * a : 256 * (a + 1)],
            (((1,), (1,)), ((), ())), preferred_element_type=F32,
        )

    load_v.wait()
    fill(win, vbuf, 1, 0, pairs)
    halves = ((0, half), (half, pairs))
    middle = [plane_fwd(1, slice(height * low, height * high)) for low, high in halves]
    load_g.wait()
    deltas, d_halos = [], []
    for piece, (low, high) in enumerate(halves):
        rows = slice(height * low, height * high)
        halo_arrive(*v_halos[piece])
        fill(win, vbuf, 0, low, high)
        fill(win, vbuf, 2, low, high)
        parts = middle[piece] + plane_fwd(0, rows) + plane_fwd(2, rows)
        pre = y_sum(parts, height)
        sig = 1.0 / (1.0 + jnp.exp(-pre))
        cot = pair_rows(gbuf[:, 128 * low : 128 * high], height, high - low).astype(F32)
        delta = (cot * sig * (1.0 + pre * (1.0 - sig))).astype(BF16)
        for k in range(low, high):
            at = slice(height * (k - low), height * (k - low + 1))
            dbuf[1, :, 128 * k : 128 * (k + 1)] = delta[at]
        d_halos.append(
            halo(dbuf.at[1], dbuf, dsend, drecv, piece, 128 * low, 128 * high)
        )
        act = (pre * sig).astype(BF16)
        for k in range(low, high):
            at = slice(height * (k - low), height * (k - low + 1))
            act_ref[0, 0, :, 128 * k : 128 * (k + 1)] = act[at]
        deltas.append(delta)
    delta = jnp.concatenate(deltas, axis=0)

    wide_delta = delta.astype(F32)
    row = lax.broadcasted_iota(jnp.int32, wide_delta.shape, 0) % height
    ahead = jnp.where(row == height - 1, 0.0, rolled(wide_delta, -1, 0)).astype(BF16)
    behind = jnp.where(row == 0, 0.0, rolled(wide_delta, 1, 0)).astype(BF16)
    moved = jnp.concatenate([ahead, delta, behind], axis=1)
    lane = lax.broadcasted_iota(jnp.int32, (64, 128), 1) < 64
    early = sum(2 * (q + 1) * rows_out <= 9 * 128 for q in range(mz))
    parts_z = ((0, early), (early, mz))
    zero_copies = []
    gathered = []
    lanes = lax.broadcasted_iota(jnp.int32, (64, 128), 1)

    def weight_terms(planes, low_z, high_z, stage):
        span = win[:, 256 * planes[0] : 256 * (planes[-1] + 1)]
        terms = lax.dot_general(
            moved, span, (((0,), (0,)), ((), ())), preferred_element_type=F32
        )
        quads = []
        for p in range(len(planes)):
            for b in range(3):
                first = terms[128 * b : 128 * b + 64, 256 * p : 256 * (p + 1)]
                second = terms[128 * b + 64 : 128 * (b + 1), 256 * p : 256 * (p + 1)]
                quads.append((first[:, :128], first[:, 128:], second[:, :128], second[:, 128:]))
        out_tiles = []
        for q in range(0, len(quads), 2):
            a1, a2, b1, b2 = quads[q]
            out_tiles.append(rolled(jnp.where(lane, a1, a2), 64, 1) + b1)
            third = rolled(a1, 64, 1) + b2
            if q + 1 == len(quads):
                out_tiles.append(jnp.where(lane, third, 0.0))
                continue
            c1, c2, e1, e2 = quads[q + 1]
            out_tiles.append(jnp.where(lane, third, c2 + rolled(e1, 64, 1)))
            out_tiles.append(c1 + rolled(jnp.where(lane, e2, e1), 64, 1))
        gathered.extend(tile * scale for tile in out_tiles)
        for g in range(2 * low_z, 2 * high_z):
            start, offset = (g * rows_out) // 128, (g * rows_out) % 128
            for j in range(wide):
                tile = gathered[start + j]
                if offset:
                    tile = rolled(tile, -offset, 1)
                    if (g + 1) * rows_out > 128 * (start + j + 1):
                        after = rolled(gathered[start + j + 1], -offset, 1)
                        tile = jnp.where(lanes < 128 - offset, tile, after)
                tile = tile.astype(BF16)
                for d in range(n):
                    part = tile[cols_out * d : cols_out * (d + 1)]
                    if cols_out % 16:
                        fill_rows = jnp.zeros((pack0.shape[4] - cols_out, 128), BF16)
                        part = jnp.concatenate([part, fill_rows], axis=0)
                    pack0[g % 2, g // 2, d, j] = part
        copy = pltpu.make_async_remote_copy(
            src_ref=pack0.at[1 - core, low_z:high_z], dst_ref=recv0.at[low_z:high_z],
            send_sem=ssend0.at[stage], recv_sem=srecv0.at[stage],
            device_id={"gz": partner}, device_id_type=MESH,
        )
        copy.start()
        zero_copies.append(copy)

    weight_terms((0, 1), 0, early, 0)
    weight_terms((2,), early, mz, 1)

    first_copies = []
    for stage, (low_z, high_z) in enumerate(parts_z):
        zero_copies[stage].wait_recv()
        both = pack0[core, low_z:high_z].astype(F32) + recv0[low_z:high_z].astype(F32)
        sum0[low_z:high_z] = both.astype(BF16)
        copies = []
        for k in range(1, n):
            peer = lax.rem(me + k, n)
            copy = pltpu.make_async_remote_copy(
                src_ref=sum0.at[low_z:high_z, peer], dst_ref=recv1.at[k - 1, low_z:high_z],
                send_sem=ssend1.at[stage, k - 1], recv_sem=srecv1.at[stage, k - 1],
                device_id={"dp": peer}, device_id_type=MESH,
            )
            copy.start()
            copies.append(copy)
        first_copies.append(copies)

    second_copies = []
    for k in range(1, mz):
        second_copies.append(pltpu.make_async_remote_copy(
            src_ref=sum1.at[lax.rem(z + k, mz)], dst_ref=recv2.at[k - 1],
            send_sem=ssend2.at[k - 1], recv_sem=srecv2.at[k - 1],
            device_id={"gz": z_peers[k - 1]}, device_id_type=MESH,
        ))
    for stage, (low_z, high_z) in enumerate(parts_z):
        total = sum0[low_z:high_z, me].astype(F32)
        for k in range(1, n):
            first_copies[stage][k - 1].wait_recv()
            total = total + recv1[k - 1, low_z:high_z].astype(F32)
        sum1[low_z:high_z] = total.astype(BF16)
        for k in range(1, mz):
            target = lax.rem(z + k, mz)

            @pl.when((target < early) if stage == 0 else (target >= early))
            def _(copy=second_copies[k - 1]):
                copy.start()

    for piece in d_halos:
        halo_arrive(*piece)
    for a in range(3):
        fill(dwin, dbuf, a, 0, pairs)
    back = jnp.dot(dwin[...], wbwd[...], preferred_element_type=F32)
    grad = y_sum(back, height).astype(BF16)
    for k in range(pairs):
        ig_ref[0, 0, :, 128 * k : 128 * (k + 1)] = grad[height * k : height * (k + 1)]

    for piece in v_halos + d_halos:
        halo_sent(*piece)
    for copy in zero_copies + first_copies[0] + first_copies[1]:
        copy.wait_send()
    total = sum1[z].astype(F32)
    for k in range(1, mz):
        second_copies[k - 1].wait_recv()
        total = total + recv2[k - 1].astype(F32)
    for t in range(wide):
        count = min(128, rows_out - 128 * t)
        wg_ref[:, 128 * t : 128 * t + count] = total[t, :cols_out, :count]
    for copy in second_copies:
        copy.wait_send()


def place(a_ref, i_ref, w_ref, act_ref, ig_ref, wg_ref, sem):
    pairs = ((a_ref, act_ref), (i_ref, ig_ref), (w_ref, wg_ref))
    copies = [pltpu.make_async_copy(a, b, sem.at[k]) for k, (a, b) in enumerate(pairs)]
    for copy in copies:
        copy.start()
    for copy in copies:
        copy.wait()


def per_device(volume, weight, cotangent):
    n = lax.axis_size("dp")
    m = lax.axis_size("gz")
    chans = weight.shape[1]
    universes, planes, height, merged = volume.shape
    assert chans == 64 and universes == 1 and planes == 1
    pairs = merged // 128
    cells = height * pairs * 2
    rows_out = weight.shape[0] // m
    cols_out = chans // n
    padded = -(-cols_out // 16) * 16
    wide = -(-rows_out // 128)
    assert 27 * 64 == weight.shape[0]
    scale = 1.0 / math.sqrt(n * m * cells)
    geom = (n, m, height, pairs, rows_out, cols_out, wide, scale)
    vmem = pltpu.VMEM
    dma = pltpu.SemaphoreType.DMA
    block = (height, merged)
    grid_rows = pairs * height
    results = pl.pallas_call(
        functools.partial(kernel, geom),
        out_shape=(
            vmem(volume.shape, BF16),
            vmem(volume.shape, BF16),
            vmem((cols_out, rows_out), F32),
        ),
        in_specs=[pl.BlockSpec(memory_space=pltpu.HBM)] * 3,
        out_specs=[pl.BlockSpec(memory_space=pltpu.VMEM)] * 3,
        scratch_shapes=[
            vmem((3, *block), BF16),
            vmem(block, BF16),
            vmem(weight.shape[::-1], BF16),
            vmem((3, *block), BF16),
            vmem((grid_rows, 768), BF16),
            vmem((grid_rows, 768), BF16),
            vmem((384, 768), BF16),
            vmem((768, 384), BF16),
            vmem((2, m // 2, n, wide, padded, 128), BF16),
            vmem((m // 2, n, wide, padded, 128), BF16),
            vmem((m // 2, n, wide, padded, 128), BF16),
            vmem((n - 1, m // 2, wide, padded, 128), BF16),
            vmem((m // 2, wide, padded, 128), BF16),
            vmem((m // 2 - 1, wide, padded, 128), BF16),
            dma((3,)), dma((2, 2)), dma((2, 2)), dma((2, 2)), dma((2, 2)),
            dma((2,)), dma((2,)), dma((2, n - 1)), dma((2, n - 1)),
            dma((m // 2 - 1,)), dma((m // 2 - 1,)),
        ],
        compiler_params=pltpu.CompilerParams(
            collective_id=0, has_side_effects=True, vmem_limit_bytes=32 * 1024 * 1024
        ),
    )(*(pltpu.with_memory_space_constraint(x, pltpu.HBM) for x in (volume, weight.T, cotangent)))
    activation, input_grad, weight_grad = pl.pallas_call(
        place,
        out_shape=tuple(jax.ShapeDtypeStruct(r.shape, r.dtype) for r in results),
        in_specs=[pl.BlockSpec(memory_space=pl.ANY)] * 3,
        out_specs=[pl.BlockSpec(memory_space=pl.ANY)] * 3,
        scratch_shapes=[dma((3,))],
        compiler_params=pltpu.CompilerParams(vmem_limit_bytes=1024 * 1024),
    )(*results)
    return activation, input_grad, weight_grad.T


def solution(mesh):
    return jax.shard_map(
        per_device,
        mesh=mesh,
        in_specs=(P("gz", "dp", None, None), P(), P("gz", "dp", None, None)),
        out_specs=(P("gz", "dp", None, None), P("gz", "dp", None, None), P("gz", "dp")),
        check_vma=False,
    )
```

```python
import functools
import math

import jax
import jax.numpy as jnp
from jax import lax
from jax.experimental import pallas as pl
from jax.experimental.pallas import tpu as pltpu
from jax.sharding import PartitionSpec as P

MESH = pl.DeviceIdType.MESH
BF16 = jnp.bfloat16
F32 = jnp.float32


def rolled(x, shift, axis):
    return pltpu.roll(x, shift % x.shape[axis], axis)


def pair_rows(plane, height, pairs):
    return jnp.concatenate([plane[:, 128 * k : 128 * (k + 1)] for k in range(pairs)], axis=0)


def windows(buf, a, height, low, high):
    zero = jnp.zeros((height, 128), buf.dtype)
    count = buf.shape[2] // 128

    def column(k):
        return buf[a, :, 128 * k : 128 * (k + 1)] if 0 <= k < count else zero

    own, after, before = (
        jnp.concatenate([column(k + shift) for k in range(low, high)], axis=0)
        for shift in (0, 1, -1)
    )
    lane = lax.broadcasted_iota(jnp.int32, own.shape, 1)
    return own, jnp.where(lane < 64, after, before)


def y_sum(parts, height):
    row = lax.broadcasted_iota(jnp.int32, (parts.shape[0], 128), 0) % height
    low = jnp.where(row == 0, 0.0, rolled(parts[:, 0:128], 1, 0))
    high = jnp.where(row == height - 1, 0.0, rolled(parts[:, 256:384], -1, 0))
    return parts[:, 128:256] + low + high


def kernel(
    geom, v_ref, w_ref, g_ref, act_ref, ig_ref, wg_ref,
    vbuf, gbuf, wbuf, dbuf, win, dwin, wfwd, wbwd,
    pack0, recv0, sum0, recv1, sum1, recv2,
    local_sem, vsend, vrecv, dsend, drecv, ssend0, srecv0, ssend1, srecv1, ssend2, srecv2,
):
    n, m, height, pairs, rows_out, cols_out, wide, scale = geom
    me = lax.axis_index("dp")
    my = lax.axis_index("gz")
    mz = m // 2
    z, core = lax.div(my, 2), lax.rem(my, 2)
    partner = my + 1 - 2 * core
    z_peers = [2 * lax.rem(z + k, mz) + core for k in range(1, mz)]

    barrier = pltpu.get_barrier_semaphore()
    for k in range(1, n):
        pl.semaphore_signal(
            barrier, inc=1, device_id={"dp": lax.rem(me + k, n)}, device_id_type=MESH
        )
    for peer in [partner] + z_peers:
        pl.semaphore_signal(barrier, inc=1, device_id={"gz": peer}, device_id_type=MESH)
    load_w = pltpu.make_async_copy(w_ref, wbuf, local_sem.at[0])
    load_v = pltpu.make_async_copy(v_ref.at[0, 0], vbuf.at[1], local_sem.at[1])
    load_g = pltpu.make_async_copy(g_ref.at[0, 0], gbuf, local_sem.at[2])
    load_w.start()
    load_v.start()
    load_g.start()
    pl.semaphore_wait(barrier, n + mz - 1)

    def halo(source, buf, ssem, rsem, piece, low, high):
        up = pltpu.make_async_remote_copy(
            src_ref=source.at[:, low:high], dst_ref=buf.at[0, :, low:high],
            send_sem=ssem.at[piece, 0], recv_sem=rsem.at[piece, 0],
            device_id={"dp": lax.rem(me + 1, n)}, device_id_type=MESH,
        )
        down = pltpu.make_async_remote_copy(
            src_ref=source.at[:, low:high], dst_ref=buf.at[2, :, low:high],
            send_sem=ssem.at[piece, 1], recv_sem=rsem.at[piece, 1],
            device_id={"dp": lax.rem(me + n - 1, n)}, device_id_type=MESH,
        )

        @pl.when(me < n - 1)
        def _():
            up.start()

        @pl.when(me > 0)
        def _():
            down.start()

        return up, down, buf, low, high

    def halo_arrive(up, down, buf, low, high):
        @pl.when(me > 0)
        def _():
            up.wait_recv()

        @pl.when(me == 0)
        def _():
            buf[0, :, low:high] = jnp.zeros((height, high - low), buf.dtype)

        @pl.when(me < n - 1)
        def _():
            down.wait_recv()

        @pl.when(me == n - 1)
        def _():
            buf[2, :, low:high] = jnp.zeros((height, high - low), buf.dtype)

    def halo_sent(up, down, *_):
        @pl.when(me < n - 1)
        def _():
            up.wait_send()

        @pl.when(me > 0)
        def _():
            down.wait_send()

    half = pairs // 2
    cut = 128 * (half + 1)
    v_halos = [
        halo(v_ref.at[0, 0], vbuf, vsend, vrecv, piece, low, high)
        for piece, (low, high) in enumerate(((0, cut), (cut, 128 * pairs)))
    ]

    load_w.wait()
    zero = jnp.zeros((64, 64), BF16)
    for a in range(3):
        for b in range(3):
            base = (a * 9 + b * 3) * 64
            k0, k1, k2 = (wbuf[:, base + 64 * c : base + 64 * (c + 1)] for c in range(3))
            top = jnp.concatenate([k1, k2, zero, k0], axis=1)
            bottom = jnp.concatenate([k0, k1, k2, zero], axis=1)
            wfwd[128 * b : 128 * (b + 1), 256 * a : 256 * (a + 1)] = jnp.concatenate(
                [top, bottom], axis=0
            )

    def fill(target, buf, a, low, high):
        own, edge = windows(buf, a, height, low, high)
        target[height * low : height * high, 256 * a : 256 * a + 128] = own
        target[height * low : height * high, 256 * a + 128 : 256 * (a + 1)] = edge

    def plane_fwd(a, rows):
        return lax.dot_general(
            win[rows, 256 * a : 256 * (a + 1)], wfwd[:, 256 * a : 256 * (a + 1)],
            (((1,), (1,)), ((), ())), preferred_element_type=F32,
        )

    load_v.wait()
    fill(win, vbuf, 1, 0, pairs)
    halves = ((0, half), (half, pairs))
    middle = [plane_fwd(1, slice(height * low, height * high)) for low, high in halves]
    load_g.wait()
    deltas, d_halos, acts = [], [], []
    for piece, (low, high) in enumerate(halves):
        rows = slice(height * low, height * high)
        halo_arrive(*v_halos[piece])
        fill(win, vbuf, 0, low, high)
        fill(win, vbuf, 2, low, high)
        parts = middle[piece] + plane_fwd(0, rows) + plane_fwd(2, rows)
        pre = y_sum(parts, height)
        sig = 1.0 / (1.0 + jnp.exp(-pre))
        cot = pair_rows(gbuf[:, 128 * low : 128 * high], height, high - low).astype(F32)
        delta = (cot * sig * (1.0 + pre * (1.0 - sig))).astype(BF16)
        for k in range(low, high):
            at = slice(height * (k - low), height * (k - low + 1))
            dbuf[1, :, 128 * k : 128 * (k + 1)] = delta[at]
        d_halos.append(
            halo(dbuf.at[1], dbuf, dsend, drecv, piece, 128 * low, 128 * high)
        )
        acts.append((pre * sig).astype(BF16))
        deltas.append(delta)
    delta = jnp.concatenate(deltas, axis=0)

    wide_delta = delta.astype(F32)
    row = lax.broadcasted_iota(jnp.int32, wide_delta.shape, 0) % height
    ahead = jnp.where(row == height - 1, 0.0, rolled(wide_delta, -1, 0)).astype(BF16)
    behind = jnp.where(row == 0, 0.0, rolled(wide_delta, 1, 0)).astype(BF16)
    moved = jnp.concatenate([ahead, delta, behind], axis=1)
    lane = lax.broadcasted_iota(jnp.int32, (64, 128), 1) < 64
    early = sum(2 * (q + 1) * rows_out <= 9 * 128 for q in range(mz))
    parts_z = ((0, early), (early, mz))
    zero_copies = []
    gathered = []
    lanes = lax.broadcasted_iota(jnp.int32, (64, 128), 1)

    def weight_terms(planes, low_z, high_z, stage):
        span = win[:, 256 * planes[0] : 256 * (planes[-1] + 1)]
        terms = lax.dot_general(
            moved, span, (((0,), (0,)), ((), ())), preferred_element_type=F32
        )
        quads = []
        for p in range(len(planes)):
            for b in range(3):
                first = terms[128 * b : 128 * b + 64, 256 * p : 256 * (p + 1)]
                second = terms[128 * b + 64 : 128 * (b + 1), 256 * p : 256 * (p + 1)]
                quads.append((first[:, :128], first[:, 128:], second[:, :128], second[:, 128:]))
        out_tiles = []
        for q in range(0, len(quads), 2):
            a1, a2, b1, b2 = quads[q]
            out_tiles.append(rolled(jnp.where(lane, a1, a2), 64, 1) + b1)
            third = rolled(a1, 64, 1) + b2
            if q + 1 == len(quads):
                out_tiles.append(jnp.where(lane, third, 0.0))
                continue
            c1, c2, e1, e2 = quads[q + 1]
            out_tiles.append(jnp.where(lane, third, c2 + rolled(e1, 64, 1)))
            out_tiles.append(c1 + rolled(jnp.where(lane, e2, e1), 64, 1))
        gathered.extend(tile * scale for tile in out_tiles)
        for g in range(2 * low_z, 2 * high_z):
            start, offset = (g * rows_out) // 128, (g * rows_out) % 128
            for j in range(wide):
                tile = gathered[start + j]
                if offset:
                    tile = rolled(tile, -offset, 1)
                    if (g + 1) * rows_out > 128 * (start + j + 1):
                        after = rolled(gathered[start + j + 1], -offset, 1)
                        tile = jnp.where(lanes < 128 - offset, tile, after)
                tile = tile.astype(BF16)
                for d in range(n):
                    part = tile[cols_out * d : cols_out * (d + 1)]
                    if cols_out % 16:
                        fill_rows = jnp.zeros((pack0.shape[4] - cols_out, 128), BF16)
                        part = jnp.concatenate([part, fill_rows], axis=0)
                    pack0[g % 2, g // 2, d, j] = part
        copy = pltpu.make_async_remote_copy(
            src_ref=pack0.at[1 - core, low_z:high_z], dst_ref=recv0.at[low_z:high_z],
            send_sem=ssend0.at[stage], recv_sem=srecv0.at[stage],
            device_id={"gz": partner}, device_id_type=MESH,
        )
        copy.start()
        zero_copies.append(copy)

    weight_terms((0, 1), 0, early, 0)
    weight_terms((2,), early, mz, 1)

    for (low, high), act in zip(halves, acts):
        for k in range(low, high):
            at = slice(height * (k - low), height * (k - low + 1))
            act_ref[0, 0, :, 128 * k : 128 * (k + 1)] = act[at]
    for a in range(3):
        for b in range(3):
            base = (a * 9 + b * 3) * 64
            k0, k1, k2 = (wbuf[:, base + 64 * c : base + 64 * (c + 1)] for c in range(3))
            left = jnp.concatenate([k1, k0, zero, k2], axis=0)
            right = jnp.concatenate([k2, k1, k0, zero], axis=0)
            fa, fb = 2 - a, 2 - b
            wbwd[256 * fa : 256 * (fa + 1), 128 * fb : 128 * (fb + 1)] = jnp.concatenate(
                [left, right], axis=1
            )
    first_copies = []
    for stage, (low_z, high_z) in enumerate(parts_z):
        zero_copies[stage].wait_recv()
        both = pack0[core, low_z:high_z].astype(F32) + recv0[low_z:high_z].astype(F32)
        sum0[low_z:high_z] = both.astype(BF16)
        copies = []
        for k in range(1, n):
            peer = lax.rem(me + k, n)
            copy = pltpu.make_async_remote_copy(
                src_ref=sum0.at[low_z:high_z, peer], dst_ref=recv1.at[k - 1, low_z:high_z],
                send_sem=ssend1.at[stage, k - 1], recv_sem=srecv1.at[stage, k - 1],
                device_id={"dp": peer}, device_id_type=MESH,
            )
            copy.start()
            copies.append(copy)
        first_copies.append(copies)

    fill(dwin, dbuf, 1, 0, pairs)
    back = jnp.dot(dwin[:, 256:512], wbwd[256:512, :], preferred_element_type=F32)
    second_copies = []
    for k in range(1, mz):
        second_copies.append(pltpu.make_async_remote_copy(
            src_ref=sum1.at[lax.rem(z + k, mz)], dst_ref=recv2.at[k - 1],
            send_sem=ssend2.at[k - 1], recv_sem=srecv2.at[k - 1],
            device_id={"gz": z_peers[k - 1]}, device_id_type=MESH,
        ))
    for stage, (low_z, high_z) in enumerate(parts_z):
        total = sum0[low_z:high_z, me].astype(F32)
        for k in range(1, n):
            first_copies[stage][k - 1].wait_recv()
            total = total + recv1[k - 1, low_z:high_z].astype(F32)
        sum1[low_z:high_z] = total.astype(BF16)
        for k in range(1, mz):
            target = lax.rem(z + k, mz)

            @pl.when((target < early) if stage == 0 else (target >= early))
            def _(copy=second_copies[k - 1]):
                copy.start()

    for piece in d_halos:
        halo_arrive(*piece)
    for a in (0, 2):
        fill(dwin, dbuf, a, 0, pairs)
        back = back + jnp.dot(
            dwin[:, 256 * a : 256 * (a + 1)], wbwd[256 * a : 256 * (a + 1), :],
            preferred_element_type=F32,
        )
    grad = y_sum(back, height).astype(BF16)
    for k in range(pairs):
        ig_ref[0, 0, :, 128 * k : 128 * (k + 1)] = grad[height * k : height * (k + 1)]

    for piece in v_halos + d_halos:
        halo_sent(*piece)
    for copy in zero_copies + first_copies[0] + first_copies[1]:
        copy.wait_send()
    total = sum1[z].astype(F32)
    for k in range(1, mz):
        second_copies[k - 1].wait_recv()
        total = total + recv2[k - 1].astype(F32)
    for t in range(wide):
        count = min(128, rows_out - 128 * t)
        wg_ref[:, 128 * t : 128 * t + count] = total[t, :cols_out, :count]
    for copy in second_copies:
        copy.wait_send()


def place(a_ref, i_ref, w_ref, act_ref, ig_ref, wg_ref, sem):
    pairs = ((a_ref, act_ref), (i_ref, ig_ref), (w_ref, wg_ref))
    copies = [pltpu.make_async_copy(a, b, sem.at[k]) for k, (a, b) in enumerate(pairs)]
    for copy in copies:
        copy.start()
    for copy in copies:
        copy.wait()


def per_device(volume, weight, cotangent):
    n = lax.axis_size("dp")
    m = lax.axis_size("gz")
    chans = weight.shape[1]
    universes, planes, height, merged = volume.shape
    assert chans == 64 and universes == 1 and planes == 1
    pairs = merged // 128
    cells = height * pairs * 2
    rows_out = weight.shape[0] // m
    cols_out = chans // n
    padded = -(-cols_out // 16) * 16
    wide = -(-rows_out // 128)
    assert 27 * 64 == weight.shape[0]
    scale = 1.0 / math.sqrt(n * m * cells)
    geom = (n, m, height, pairs, rows_out, cols_out, wide, scale)
    vmem = pltpu.VMEM
    dma = pltpu.SemaphoreType.DMA
    block = (height, merged)
    grid_rows = pairs * height
    results = pl.pallas_call(
        functools.partial(kernel, geom),
        out_shape=(
            vmem(volume.shape, BF16),
            vmem(volume.shape, BF16),
            vmem((cols_out, rows_out), F32),
        ),
        in_specs=[pl.BlockSpec(memory_space=pltpu.HBM)] * 3,
        out_specs=[pl.BlockSpec(memory_space=pltpu.VMEM)] * 3,
        scratch_shapes=[
            vmem((3, *block), BF16),
            vmem(block, BF16),
            vmem(weight.shape[::-1], BF16),
            vmem((3, *block), BF16),
            vmem((grid_rows, 768), BF16),
            vmem((grid_rows, 768), BF16),
            vmem((384, 768), BF16),
            vmem((768, 384), BF16),
            vmem((2, m // 2, n, wide, padded, 128), BF16),
            vmem((m // 2, n, wide, padded, 128), BF16),
            vmem((m // 2, n, wide, padded, 128), BF16),
            vmem((n - 1, m // 2, wide, padded, 128), BF16),
            vmem((m // 2, wide, padded, 128), BF16),
            vmem((m // 2 - 1, wide, padded, 128), BF16),
            dma((3,)), dma((2, 2)), dma((2, 2)), dma((2, 2)), dma((2, 2)),
            dma((2,)), dma((2,)), dma((2, n - 1)), dma((2, n - 1)),
            dma((m // 2 - 1,)), dma((m // 2 - 1,)),
        ],
        compiler_params=pltpu.CompilerParams(
            collective_id=0, has_side_effects=True, vmem_limit_bytes=32 * 1024 * 1024
        ),
    )(*(pltpu.with_memory_space_constraint(x, pltpu.HBM) for x in (volume, weight.T, cotangent)))
    activation, input_grad, weight_grad = pl.pallas_call(
        place,
        out_shape=tuple(jax.ShapeDtypeStruct(r.shape, r.dtype) for r in results),
        in_specs=[pl.BlockSpec(memory_space=pl.ANY)] * 3,
        out_specs=[pl.BlockSpec(memory_space=pl.ANY)] * 3,
        scratch_shapes=[dma((3,))],
        compiler_params=pltpu.CompilerParams(vmem_limit_bytes=1024 * 1024),
    )(*results)
    return activation, input_grad, weight_grad.T


def solution(mesh):
    return jax.shard_map(
        per_device,
        mesh=mesh,
        in_specs=(P("gz", "dp", None, None), P(), P("gz", "dp", None, None)),
        out_specs=(P("gz", "dp", None, None), P("gz", "dp", None, None), P("gz", "dp")),
        check_vma=False,
    )
```

```python
import functools
import math

import jax
import jax.numpy as jnp
from jax import lax
from jax.experimental import pallas as pl
from jax.experimental.pallas import tpu as pltpu
from jax.sharding import PartitionSpec as P

MESH = pl.DeviceIdType.MESH
BF16 = jnp.bfloat16
F32 = jnp.float32


def rolled(x, shift, axis):
    return pltpu.roll(x, shift % x.shape[axis], axis)


def pair_rows(plane, height, pairs):
    return jnp.concatenate([plane[:, 128 * k : 128 * (k + 1)] for k in range(pairs)], axis=0)


def windows(buf, a, height, low, high):
    zero = jnp.zeros((height, 128), buf.dtype)
    count = buf.shape[2] // 128

    def column(k):
        return buf[a, :, 128 * k : 128 * (k + 1)] if 0 <= k < count else zero

    own, after, before = (
        jnp.concatenate([column(k + shift) for k in range(low, high)], axis=0)
        for shift in (0, 1, -1)
    )
    lane = lax.broadcasted_iota(jnp.int32, own.shape, 1)
    return own, jnp.where(lane < 64, after, before)


def y_sum(parts, height):
    row = lax.broadcasted_iota(jnp.int32, (parts.shape[0], 128), 0) % height
    low = jnp.where(row == 0, 0.0, rolled(parts[:, 0:128], 1, 0))
    high = jnp.where(row == height - 1, 0.0, rolled(parts[:, 256:384], -1, 0))
    return parts[:, 128:256] + low + high


def kernel(
    geom, v_ref, w_ref, g_ref, act_ref, ig_ref, wg_ref,
    vbuf, gbuf, wbuf, dbuf, win, dwin, wfwd, wbwd,
    pack0, recv0, sum0, recv1, sum1, recv2,
    local_sem, vsend, vrecv, dsend, drecv, ssend0, srecv0, ssend1, srecv1, ssend2, srecv2,
):
    n, m, height, pairs, rows_out, cols_out, wide, scale = geom
    me = lax.axis_index("dp")
    my = lax.axis_index("gz")
    mz = m // 2
    z, core = lax.div(my, 2), lax.rem(my, 2)
    partner = my + 1 - 2 * core
    z_peers = [2 * lax.rem(z + k, mz) + core for k in range(1, mz)]

    barrier = pltpu.get_barrier_semaphore()
    for k in range(1, n):
        pl.semaphore_signal(
            barrier, inc=1, device_id={"dp": lax.rem(me + k, n)}, device_id_type=MESH
        )
    for peer in [partner] + z_peers:
        pl.semaphore_signal(barrier, inc=1, device_id={"gz": peer}, device_id_type=MESH)
    load_w = pltpu.make_async_copy(w_ref, wbuf, local_sem.at[0])
    load_v = pltpu.make_async_copy(v_ref.at[0, 0], vbuf.at[1], local_sem.at[1])
    load_g = pltpu.make_async_copy(g_ref.at[0, 0], gbuf, local_sem.at[2])
    load_w.start()
    load_v.start()
    load_g.start()
    pl.semaphore_wait(barrier, n + mz - 1)

    def halo(source, buf, ssem, rsem, piece, low, high):
        up = pltpu.make_async_remote_copy(
            src_ref=source.at[:, low:high], dst_ref=buf.at[0, :, low:high],
            send_sem=ssem.at[piece, 0], recv_sem=rsem.at[piece, 0],
            device_id={"dp": lax.rem(me + 1, n)}, device_id_type=MESH,
        )
        down = pltpu.make_async_remote_copy(
            src_ref=source.at[:, low:high], dst_ref=buf.at[2, :, low:high],
            send_sem=ssem.at[piece, 1], recv_sem=rsem.at[piece, 1],
            device_id={"dp": lax.rem(me + n - 1, n)}, device_id_type=MESH,
        )

        @pl.when(me < n - 1)
        def _():
            up.start()

        @pl.when(me > 0)
        def _():
            down.start()

        return up, down, buf, low, high

    def halo_arrive(up, down, buf, low, high):
        @pl.when(me > 0)
        def _():
            up.wait_recv()

        @pl.when(me == 0)
        def _():
            buf[0, :, low:high] = jnp.zeros((height, high - low), buf.dtype)

        @pl.when(me < n - 1)
        def _():
            down.wait_recv()

        @pl.when(me == n - 1)
        def _():
            buf[2, :, low:high] = jnp.zeros((height, high - low), buf.dtype)

    def halo_sent(up, down, *_):
        @pl.when(me < n - 1)
        def _():
            up.wait_send()

        @pl.when(me > 0)
        def _():
            down.wait_send()

    half = pairs // 2
    cut = 128 * (half + 1)
    v_halos = [
        halo(v_ref.at[0, 0], vbuf, vsend, vrecv, piece, low, high)
        for piece, (low, high) in enumerate(((0, cut), (cut, 128 * pairs)))
    ]

    load_w.wait()
    zero = jnp.zeros((64, 64), BF16)
    for a in range(3):
        for b in range(3):
            base = (a * 9 + b * 3) * 64
            k0, k1, k2 = (wbuf[:, base + 64 * c : base + 64 * (c + 1)] for c in range(3))
            top = jnp.concatenate([k1, k2, zero, k0], axis=1)
            bottom = jnp.concatenate([k0, k1, k2, zero], axis=1)
            wfwd[128 * b : 128 * (b + 1), 256 * a : 256 * (a + 1)] = jnp.concatenate(
                [top, bottom], axis=0
            )

    for a in range(3):
        for b in range(3):
            base = (a * 9 + b * 3) * 64
            k0, k1, k2 = (wbuf[:, base + 64 * c : base + 64 * (c + 1)] for c in range(3))
            left = jnp.concatenate([k1, k0, zero, k2], axis=0)
            right = jnp.concatenate([k2, k1, k0, zero], axis=0)
            fa, fb = 2 - a, 2 - b
            wbwd[256 * fa : 256 * (fa + 1), 128 * fb : 128 * (fb + 1)] = jnp.concatenate(
                [left, right], axis=1
            )

    def fill(target, buf, a, low, high):
        own, edge = windows(buf, a, height, low, high)
        target[height * low : height * high, 256 * a : 256 * a + 128] = own
        target[height * low : height * high, 256 * a + 128 : 256 * (a + 1)] = edge

    def plane_fwd(a, rows):
        return lax.dot_general(
            win[rows, 256 * a : 256 * (a + 1)], wfwd[:, 256 * a : 256 * (a + 1)],
            (((1,), (1,)), ((), ())), preferred_element_type=F32,
        )

    load_v.wait()
    fill(win, vbuf, 1, 0, pairs)
    halves = ((0, half), (half, pairs))
    middle = [plane_fwd(1, slice(height * low, height * high)) for low, high in halves]
    load_g.wait()
    deltas, d_halos, acts = [], [], []
    for piece, (low, high) in enumerate(halves):
        rows = slice(height * low, height * high)
        halo_arrive(*v_halos[piece])
        fill(win, vbuf, 0, low, high)
        fill(win, vbuf, 2, low, high)
        parts = middle[piece] + plane_fwd(0, rows) + plane_fwd(2, rows)
        pre = y_sum(parts, height)
        sig = 1.0 / (1.0 + jnp.exp(-pre))
        cot = pair_rows(gbuf[:, 128 * low : 128 * high], height, high - low).astype(F32)
        delta = (cot * sig * (1.0 + pre * (1.0 - sig))).astype(BF16)
        for k in range(low, high):
            at = slice(height * (k - low), height * (k - low + 1))
            dbuf[1, :, 128 * k : 128 * (k + 1)] = delta[at]
        d_halos.append(
            halo(dbuf.at[1], dbuf, dsend, drecv, piece, 128 * low, 128 * high)
        )
        acts.append((pre * sig).astype(BF16))
        deltas.append(delta)
    delta = jnp.concatenate(deltas, axis=0)

    wide_delta = delta.astype(F32)
    row = lax.broadcasted_iota(jnp.int32, wide_delta.shape, 0) % height
    ahead = jnp.where(row == height - 1, 0.0, rolled(wide_delta, -1, 0)).astype(BF16)
    behind = jnp.where(row == 0, 0.0, rolled(wide_delta, 1, 0)).astype(BF16)
    moved = jnp.concatenate([ahead, delta, behind], axis=1)
    lane = lax.broadcasted_iota(jnp.int32, (64, 128), 1) < 64
    early = sum(2 * (q + 1) * rows_out <= 9 * 128 for q in range(mz))
    parts_z = ((0, early), (early, mz))
    zero_copies = []
    gathered = []
    lanes = lax.broadcasted_iota(jnp.int32, (64, 128), 1)

    def weight_terms(planes, low_z, high_z, stage):
        span = win[:, 256 * planes[0] : 256 * (planes[-1] + 1)]
        terms = lax.dot_general(
            moved, span, (((0,), (0,)), ((), ())), preferred_element_type=F32
        )
        quads = []
        for p in range(len(planes)):
            for b in range(3):
                first = terms[128 * b : 128 * b + 64, 256 * p : 256 * (p + 1)]
                second = terms[128 * b + 64 : 128 * (b + 1), 256 * p : 256 * (p + 1)]
                quads.append((first[:, :128], first[:, 128:], second[:, :128], second[:, 128:]))
        out_tiles = []
        for q in range(0, len(quads), 2):
            a1, a2, b1, b2 = quads[q]
            out_tiles.append(rolled(jnp.where(lane, a1, a2), 64, 1) + b1)
            third = rolled(a1, 64, 1) + b2
            if q + 1 == len(quads):
                out_tiles.append(jnp.where(lane, third, 0.0))
                continue
            c1, c2, e1, e2 = quads[q + 1]
            out_tiles.append(jnp.where(lane, third, c2 + rolled(e1, 64, 1)))
            out_tiles.append(c1 + rolled(jnp.where(lane, e2, e1), 64, 1))
        gathered.extend(tile * scale for tile in out_tiles)
        for g in range(2 * low_z, 2 * high_z):
            start, offset = (g * rows_out) // 128, (g * rows_out) % 128
            for j in range(wide):
                tile = gathered[start + j]
                if offset:
                    tile = rolled(tile, -offset, 1)
                    if (g + 1) * rows_out > 128 * (start + j + 1):
                        after = rolled(gathered[start + j + 1], -offset, 1)
                        tile = jnp.where(lanes < 128 - offset, tile, after)
                tile = tile.astype(BF16)
                for d in range(n):
                    part = tile[cols_out * d : cols_out * (d + 1)]
                    if cols_out % 16:
                        fill_rows = jnp.zeros((pack0.shape[4] - cols_out, 128), BF16)
                        part = jnp.concatenate([part, fill_rows], axis=0)
                    pack0[g % 2, g // 2, d, j] = part
        copy = pltpu.make_async_remote_copy(
            src_ref=pack0.at[1 - core, low_z:high_z], dst_ref=recv0.at[low_z:high_z],
            send_sem=ssend0.at[stage], recv_sem=srecv0.at[stage],
            device_id={"gz": partner}, device_id_type=MESH,
        )
        copy.start()
        zero_copies.append(copy)

    weight_terms((0, 1), 0, early, 0)
    weight_terms((2,), early, mz, 1)

    first_copies = []
    for stage, (low_z, high_z) in enumerate(parts_z):
        zero_copies[stage].wait_recv()
        both = pack0[core, low_z:high_z].astype(F32) + recv0[low_z:high_z].astype(F32)
        sum0[low_z:high_z] = both.astype(BF16)
        copies = []
        for k in range(1, n):
            peer = lax.rem(me + k, n)
            copy = pltpu.make_async_remote_copy(
                src_ref=sum0.at[low_z:high_z, peer], dst_ref=recv1.at[k - 1, low_z:high_z],
                send_sem=ssend1.at[stage, k - 1], recv_sem=srecv1.at[stage, k - 1],
                device_id={"dp": peer}, device_id_type=MESH,
            )
            copy.start()
            copies.append(copy)
        first_copies.append(copies)

    for (low, high), act in zip(halves, acts):
        for k in range(low, high):
            at = slice(height * (k - low), height * (k - low + 1))
            act_ref[0, 0, :, 128 * k : 128 * (k + 1)] = act[at]
    fill(dwin, dbuf, 1, 0, pairs)
    back = jnp.dot(dwin[:, 256:512], wbwd[256:512, :], preferred_element_type=F32)
    second_copies = []
    for k in range(1, mz):
        second_copies.append(pltpu.make_async_remote_copy(
            src_ref=sum1.at[lax.rem(z + k, mz)], dst_ref=recv2.at[k - 1],
            send_sem=ssend2.at[k - 1], recv_sem=srecv2.at[k - 1],
            device_id={"gz": z_peers[k - 1]}, device_id_type=MESH,
        ))
    for stage, (low_z, high_z) in enumerate(parts_z):
        total = sum0[low_z:high_z, me].astype(F32)
        for k in range(1, n):
            first_copies[stage][k - 1].wait_recv()
            total = total + recv1[k - 1, low_z:high_z].astype(F32)
        sum1[low_z:high_z] = total.astype(BF16)
        for k in range(1, mz):
            target = lax.rem(z + k, mz)

            @pl.when((target < early) if stage == 0 else (target >= early))
            def _(copy=second_copies[k - 1]):
                copy.start()

    for piece in d_halos:
        halo_arrive(*piece)
    for a in (0, 2):
        fill(dwin, dbuf, a, 0, pairs)
        back = back + jnp.dot(
            dwin[:, 256 * a : 256 * (a + 1)], wbwd[256 * a : 256 * (a + 1), :],
            preferred_element_type=F32,
        )
    grad = y_sum(back, height).astype(BF16)
    for k in range(pairs):
        ig_ref[0, 0, :, 128 * k : 128 * (k + 1)] = grad[height * k : height * (k + 1)]

    for piece in v_halos + d_halos:
        halo_sent(*piece)
    for copy in zero_copies + first_copies[0] + first_copies[1]:
        copy.wait_send()
    total = sum1[z].astype(F32)
    for k in range(1, mz):
        second_copies[k - 1].wait_recv()
        total = total + recv2[k - 1].astype(F32)
    for t in range(wide):
        count = min(128, rows_out - 128 * t)
        wg_ref[:, 128 * t : 128 * t + count] = total[t, :cols_out, :count]
    for copy in second_copies:
        copy.wait_send()


def place(a_ref, i_ref, w_ref, act_ref, ig_ref, wg_ref, sem):
    pairs = ((a_ref, act_ref), (i_ref, ig_ref), (w_ref, wg_ref))
    copies = [pltpu.make_async_copy(a, b, sem.at[k]) for k, (a, b) in enumerate(pairs)]
    for copy in copies:
        copy.start()
    for copy in copies:
        copy.wait()


def per_device(volume, weight, cotangent):
    n = lax.axis_size("dp")
    m = lax.axis_size("gz")
    chans = weight.shape[1]
    universes, planes, height, merged = volume.shape
    assert chans == 64 and universes == 1 and planes == 1
    pairs = merged // 128
    cells = height * pairs * 2
    rows_out = weight.shape[0] // m
    cols_out = chans // n
    padded = -(-cols_out // 16) * 16
    wide = -(-rows_out // 128)
    assert 27 * 64 == weight.shape[0]
    scale = 1.0 / math.sqrt(n * m * cells)
    geom = (n, m, height, pairs, rows_out, cols_out, wide, scale)
    vmem = pltpu.VMEM
    dma = pltpu.SemaphoreType.DMA
    block = (height, merged)
    grid_rows = pairs * height
    results = pl.pallas_call(
        functools.partial(kernel, geom),
        out_shape=(
            vmem(volume.shape, BF16),
            vmem(volume.shape, BF16),
            vmem((cols_out, rows_out), F32),
        ),
        in_specs=[pl.BlockSpec(memory_space=pltpu.HBM)] * 3,
        out_specs=[pl.BlockSpec(memory_space=pltpu.VMEM)] * 3,
        scratch_shapes=[
            vmem((3, *block), BF16),
            vmem(block, BF16),
            vmem(weight.shape[::-1], BF16),
            vmem((3, *block), BF16),
            vmem((grid_rows, 768), BF16),
            vmem((grid_rows, 768), BF16),
            vmem((384, 768), BF16),
            vmem((768, 384), BF16),
            vmem((2, m // 2, n, wide, padded, 128), BF16),
            vmem((m // 2, n, wide, padded, 128), BF16),
            vmem((m // 2, n, wide, padded, 128), BF16),
            vmem((n - 1, m // 2, wide, padded, 128), BF16),
            vmem((m // 2, wide, padded, 128), BF16),
            vmem((m // 2 - 1, wide, padded, 128), BF16),
            dma((3,)), dma((2, 2)), dma((2, 2)), dma((2, 2)), dma((2, 2)),
            dma((2,)), dma((2,)), dma((2, n - 1)), dma((2, n - 1)),
            dma((m // 2 - 1,)), dma((m // 2 - 1,)),
        ],
        compiler_params=pltpu.CompilerParams(
            collective_id=0, has_side_effects=True, vmem_limit_bytes=32 * 1024 * 1024
        ),
    )(*(pltpu.with_memory_space_constraint(x, pltpu.HBM) for x in (volume, weight.T, cotangent)))
    activation, input_grad, weight_grad = pl.pallas_call(
        place,
        out_shape=tuple(jax.ShapeDtypeStruct(r.shape, r.dtype) for r in results),
        in_specs=[pl.BlockSpec(memory_space=pl.ANY)] * 3,
        out_specs=[pl.BlockSpec(memory_space=pl.ANY)] * 3,
        scratch_shapes=[dma((3,))],
        compiler_params=pltpu.CompilerParams(vmem_limit_bytes=1024 * 1024),
    )(*results)
    return activation, input_grad, weight_grad.T


def solution(mesh):
    return jax.shard_map(
        per_device,
        mesh=mesh,
        in_specs=(P("gz", "dp", None, None), P(), P("gz", "dp", None, None)),
        out_specs=(P("gz", "dp", None, None), P("gz", "dp", None, None), P("gz", "dp")),
        check_vma=False,
    )
```

```python
import functools
import math

import jax
import jax.numpy as jnp
from jax import lax
from jax.experimental import pallas as pl
from jax.experimental.pallas import tpu as pltpu
from jax.sharding import PartitionSpec as P

MESH = pl.DeviceIdType.MESH
BF16 = jnp.bfloat16
F32 = jnp.float32


def rolled(x, shift, axis):
    return pltpu.roll(x, shift % x.shape[axis], axis)


def pair_rows(plane, height, pairs):
    return jnp.concatenate([plane[:, 128 * k : 128 * (k + 1)] for k in range(pairs)], axis=0)


def windows(buf, a, height, low, high):
    zero = jnp.zeros((height, 128), buf.dtype)
    count = buf.shape[2] // 128

    def column(k):
        return buf[a, :, 128 * k : 128 * (k + 1)] if 0 <= k < count else zero

    own, after, before = (
        jnp.concatenate([column(k + shift) for k in range(low, high)], axis=0)
        for shift in (0, 1, -1)
    )
    lane = lax.broadcasted_iota(jnp.int32, own.shape, 1)
    return own, jnp.where(lane < 64, after, before)


def y_sum(parts, height):
    row = lax.broadcasted_iota(jnp.int32, (parts.shape[0], 128), 0) % height
    low = jnp.where(row == 0, 0.0, rolled(parts[:, 0:128], 1, 0))
    high = jnp.where(row == height - 1, 0.0, rolled(parts[:, 256:384], -1, 0))
    return parts[:, 128:256] + low + high


def kernel(
    geom, v_ref, w_ref, g_ref, act_ref, ig_ref, wg_ref,
    vbuf, gbuf, wbuf, dbuf, win, dwin, wfwd, wbwd,
    pack0, recv0, sum0, recv1, sum1, recv2,
    local_sem, vsend, vrecv, dsend, drecv, ssend0, srecv0, ssend1, srecv1, ssend2, srecv2,
):
    n, m, height, pairs, rows_out, cols_out, wide, scale = geom
    me = lax.axis_index("dp")
    my = lax.axis_index("gz")
    mz = m // 2
    z, core = lax.div(my, 2), lax.rem(my, 2)
    partner = my + 1 - 2 * core
    z_peers = [2 * lax.rem(z + k, mz) + core for k in range(1, mz)]

    barrier = pltpu.get_barrier_semaphore()
    for k in range(1, n):
        pl.semaphore_signal(
            barrier, inc=1, device_id={"dp": lax.rem(me + k, n)}, device_id_type=MESH
        )
    for peer in [partner] + z_peers:
        pl.semaphore_signal(barrier, inc=1, device_id={"gz": peer}, device_id_type=MESH)
    load_w = pltpu.make_async_copy(w_ref, wbuf, local_sem.at[0])
    load_v = pltpu.make_async_copy(v_ref.at[0, 0], vbuf.at[1], local_sem.at[1])
    load_g = pltpu.make_async_copy(g_ref.at[0, 0], gbuf, local_sem.at[2])
    load_w.start()
    load_v.start()
    load_g.start()
    pl.semaphore_wait(barrier, n + mz - 1)

    def halo(source, buf, ssem, rsem, piece, low, high):
        up = pltpu.make_async_remote_copy(
            src_ref=source.at[:, low:high], dst_ref=buf.at[0, :, low:high],
            send_sem=ssem.at[piece, 0], recv_sem=rsem.at[piece, 0],
            device_id={"dp": lax.rem(me + 1, n)}, device_id_type=MESH,
        )
        down = pltpu.make_async_remote_copy(
            src_ref=source.at[:, low:high], dst_ref=buf.at[2, :, low:high],
            send_sem=ssem.at[piece, 1], recv_sem=rsem.at[piece, 1],
            device_id={"dp": lax.rem(me + n - 1, n)}, device_id_type=MESH,
        )

        @pl.when(me < n - 1)
        def _():
            up.start()

        @pl.when(me > 0)
        def _():
            down.start()

        return up, down, buf, low, high

    def halo_arrive(up, down, buf, low, high):
        @pl.when(me > 0)
        def _():
            up.wait_recv()

        @pl.when(me == 0)
        def _():
            buf[0, :, low:high] = jnp.zeros((height, high - low), buf.dtype)

        @pl.when(me < n - 1)
        def _():
            down.wait_recv()

        @pl.when(me == n - 1)
        def _():
            buf[2, :, low:high] = jnp.zeros((height, high - low), buf.dtype)

    def halo_sent(up, down, *_):
        @pl.when(me < n - 1)
        def _():
            up.wait_send()

        @pl.when(me > 0)
        def _():
            down.wait_send()

    half = pairs // 2
    cut = 128 * (half + 1)
    v_halos = [
        halo(v_ref.at[0, 0], vbuf, vsend, vrecv, piece, low, high)
        for piece, (low, high) in enumerate(((0, cut), (cut, 128 * pairs)))
    ]

    load_w.wait()
    zero = jnp.zeros((64, 64), BF16)
    for a in range(3):
        for b in range(3):
            base = (a * 9 + b * 3) * 64
            k0, k1, k2 = (wbuf[:, base + 64 * c : base + 64 * (c + 1)] for c in range(3))
            top = jnp.concatenate([k1, k2, zero, k0], axis=1)
            bottom = jnp.concatenate([k0, k1, k2, zero], axis=1)
            wfwd[128 * b : 128 * (b + 1), 256 * a : 256 * (a + 1)] = jnp.concatenate(
                [top, bottom], axis=0
            )

    for a in range(3):
        for b in range(3):
            base = (a * 9 + b * 3) * 64
            k0, k1, k2 = (wbuf[:, base + 64 * c : base + 64 * (c + 1)] for c in range(3))
            left = jnp.concatenate([k1, k0, zero, k2], axis=0)
            right = jnp.concatenate([k2, k1, k0, zero], axis=0)
            fa, fb = 2 - a, 2 - b
            wbwd[256 * fa : 256 * (fa + 1), 128 * fb : 128 * (fb + 1)] = jnp.concatenate(
                [left, right], axis=1
            )

    def fill(target, buf, a, low, high):
        own, edge = windows(buf, a, height, low, high)
        target[height * low : height * high, 256 * a : 256 * a + 128] = own
        target[height * low : height * high, 256 * a + 128 : 256 * (a + 1)] = edge

    def plane_fwd(a, rows):
        return lax.dot_general(
            win[rows, 256 * a : 256 * (a + 1)], wfwd[:, 256 * a : 256 * (a + 1)],
            (((1,), (1,)), ((), ())), preferred_element_type=F32,
        )

    load_v.wait()
    fill(win, vbuf, 1, 0, pairs)
    halves = ((0, half), (half, pairs))
    middle = [plane_fwd(1, slice(height * low, height * high)) for low, high in halves]
    load_g.wait()
    d_halos, acts = [], []
    spans = (slice(0, 512), slice(512, 768))

    def products(left, rows, span):
        return lax.dot_general(
            left, win[rows, span], (((0,), (0,)), ((), ())), preferred_element_type=F32
        )

    for piece, (low, high) in enumerate(halves):
        rows = slice(height * low, height * high)
        halo_arrive(*v_halos[piece])
        fill(win, vbuf, 0, low, high)
        fill(win, vbuf, 2, low, high)
        parts = middle[piece] + plane_fwd(0, rows) + plane_fwd(2, rows)
        pre = y_sum(parts, height)
        sig = 1.0 / (1.0 + jnp.exp(-pre))
        cot = pair_rows(gbuf[:, 128 * low : 128 * high], height, high - low).astype(F32)
        delta = (cot * sig * (1.0 + pre * (1.0 - sig))).astype(BF16)
        for k in range(low, high):
            at = slice(height * (k - low), height * (k - low + 1))
            dbuf[1, :, 128 * k : 128 * (k + 1)] = delta[at]
        d_halos.append(
            halo(dbuf.at[1], dbuf, dsend, drecv, piece, 128 * low, 128 * high)
        )
        acts.append((pre * sig).astype(BF16))
        wide_delta = delta.astype(F32)
        row = lax.broadcasted_iota(jnp.int32, wide_delta.shape, 0) % height
        ahead = jnp.where(row == height - 1, 0.0, rolled(wide_delta, -1, 0)).astype(BF16)
        behind = jnp.where(row == 0, 0.0, rolled(wide_delta, 1, 0)).astype(BF16)
        moved = jnp.concatenate([ahead, delta, behind], axis=1)
        if piece == 0:
            first_terms = [products(moved, rows, span) for span in spans]

    lane = lax.broadcasted_iota(jnp.int32, (64, 128), 1) < 64
    early = sum(2 * (q + 1) * rows_out <= 9 * 128 for q in range(mz))
    parts_z = ((0, early), (early, mz))
    zero_copies = []
    gathered = []
    lanes = lax.broadcasted_iota(jnp.int32, (64, 128), 1)

    def weight_terms(planes, low_z, high_z, stage):
        terms = first_terms[stage] + products(moved, rows, spans[stage])
        quads = []
        for p in range(len(planes)):
            for b in range(3):
                first = terms[128 * b : 128 * b + 64, 256 * p : 256 * (p + 1)]
                second = terms[128 * b + 64 : 128 * (b + 1), 256 * p : 256 * (p + 1)]
                quads.append((first[:, :128], first[:, 128:], second[:, :128], second[:, 128:]))
        out_tiles = []
        for q in range(0, len(quads), 2):
            a1, a2, b1, b2 = quads[q]
            out_tiles.append(rolled(jnp.where(lane, a1, a2), 64, 1) + b1)
            third = rolled(a1, 64, 1) + b2
            if q + 1 == len(quads):
                out_tiles.append(jnp.where(lane, third, 0.0))
                continue
            c1, c2, e1, e2 = quads[q + 1]
            out_tiles.append(jnp.where(lane, third, c2 + rolled(e1, 64, 1)))
            out_tiles.append(c1 + rolled(jnp.where(lane, e2, e1), 64, 1))
        gathered.extend(tile * scale for tile in out_tiles)
        for g in range(2 * low_z, 2 * high_z):
            start, offset = (g * rows_out) // 128, (g * rows_out) % 128
            for j in range(wide):
                tile = gathered[start + j]
                if offset:
                    tile = rolled(tile, -offset, 1)
                    if (g + 1) * rows_out > 128 * (start + j + 1):
                        after = rolled(gathered[start + j + 1], -offset, 1)
                        tile = jnp.where(lanes < 128 - offset, tile, after)
                tile = tile.astype(BF16)
                for d in range(n):
                    part = tile[cols_out * d : cols_out * (d + 1)]
                    if cols_out % 16:
                        fill_rows = jnp.zeros((pack0.shape[4] - cols_out, 128), BF16)
                        part = jnp.concatenate([part, fill_rows], axis=0)
                    pack0[g % 2, g // 2, d, j] = part
        copy = pltpu.make_async_remote_copy(
            src_ref=pack0.at[1 - core, low_z:high_z], dst_ref=recv0.at[low_z:high_z],
            send_sem=ssend0.at[stage], recv_sem=srecv0.at[stage],
            device_id={"gz": partner}, device_id_type=MESH,
        )
        copy.start()
        zero_copies.append(copy)

    weight_terms((0, 1), 0, early, 0)
    weight_terms((2,), early, mz, 1)

    first_copies = []
    for stage, (low_z, high_z) in enumerate(parts_z):
        zero_copies[stage].wait_recv()
        both = pack0[core, low_z:high_z].astype(F32) + recv0[low_z:high_z].astype(F32)
        sum0[low_z:high_z] = both.astype(BF16)
        copies = []
        for k in range(1, n):
            peer = lax.rem(me + k, n)
            copy = pltpu.make_async_remote_copy(
                src_ref=sum0.at[low_z:high_z, peer], dst_ref=recv1.at[k - 1, low_z:high_z],
                send_sem=ssend1.at[stage, k - 1], recv_sem=srecv1.at[stage, k - 1],
                device_id={"dp": peer}, device_id_type=MESH,
            )
            copy.start()
            copies.append(copy)
        first_copies.append(copies)

    for (low, high), act in zip(halves, acts):
        for k in range(low, high):
            at = slice(height * (k - low), height * (k - low + 1))
            act_ref[0, 0, :, 128 * k : 128 * (k + 1)] = act[at]
    fill(dwin, dbuf, 1, 0, pairs)
    back = jnp.dot(dwin[:, 256:512], wbwd[256:512, :], preferred_element_type=F32)
    second_copies = []
    for k in range(1, mz):
        second_copies.append(pltpu.make_async_remote_copy(
            src_ref=sum1.at[lax.rem(z + k, mz)], dst_ref=recv2.at[k - 1],
            send_sem=ssend2.at[k - 1], recv_sem=srecv2.at[k - 1],
            device_id={"gz": z_peers[k - 1]}, device_id_type=MESH,
        ))
    for stage, (low_z, high_z) in enumerate(parts_z):
        total = sum0[low_z:high_z, me].astype(F32)
        for k in range(1, n):
            first_copies[stage][k - 1].wait_recv()
            total = total + recv1[k - 1, low_z:high_z].astype(F32)
        sum1[low_z:high_z] = total.astype(BF16)
        for k in range(1, mz):
            target = lax.rem(z + k, mz)

            @pl.when((target < early) if stage == 0 else (target >= early))
            def _(copy=second_copies[k - 1]):
                copy.start()

    for piece in d_halos:
        halo_arrive(*piece)
    for a in (0, 2):
        fill(dwin, dbuf, a, 0, pairs)
        back = back + jnp.dot(
            dwin[:, 256 * a : 256 * (a + 1)], wbwd[256 * a : 256 * (a + 1), :],
            preferred_element_type=F32,
        )
    grad = y_sum(back, height).astype(BF16)
    for k in range(pairs):
        ig_ref[0, 0, :, 128 * k : 128 * (k + 1)] = grad[height * k : height * (k + 1)]

    for piece in v_halos + d_halos:
        halo_sent(*piece)
    for copy in zero_copies + first_copies[0] + first_copies[1]:
        copy.wait_send()
    total = sum1[z].astype(F32)
    for k in range(1, mz):
        second_copies[k - 1].wait_recv()
        total = total + recv2[k - 1].astype(F32)
    for t in range(wide):
        count = min(128, rows_out - 128 * t)
        wg_ref[:, 128 * t : 128 * t + count] = total[t, :cols_out, :count]
    for copy in second_copies:
        copy.wait_send()


def place(a_ref, i_ref, w_ref, act_ref, ig_ref, wg_ref, sem):
    pairs = ((a_ref, act_ref), (i_ref, ig_ref), (w_ref, wg_ref))
    copies = [pltpu.make_async_copy(a, b, sem.at[k]) for k, (a, b) in enumerate(pairs)]
    for copy in copies:
        copy.start()
    for copy in copies:
        copy.wait()


def per_device(volume, weight, cotangent):
    n = lax.axis_size("dp")
    m = lax.axis_size("gz")
    chans = weight.shape[1]
    universes, planes, height, merged = volume.shape
    assert chans == 64 and universes == 1 and planes == 1
    pairs = merged // 128
    cells = height * pairs * 2
    rows_out = weight.shape[0] // m
    cols_out = chans // n
    padded = -(-cols_out // 16) * 16
    wide = -(-rows_out // 128)
    assert 27 * 64 == weight.shape[0]
    scale = 1.0 / math.sqrt(n * m * cells)
    geom = (n, m, height, pairs, rows_out, cols_out, wide, scale)
    vmem = pltpu.VMEM
    dma = pltpu.SemaphoreType.DMA
    block = (height, merged)
    grid_rows = pairs * height
    results = pl.pallas_call(
        functools.partial(kernel, geom),
        out_shape=(
            vmem(volume.shape, BF16),
            vmem(volume.shape, BF16),
            vmem((cols_out, rows_out), F32),
        ),
        in_specs=[pl.BlockSpec(memory_space=pltpu.HBM)] * 3,
        out_specs=[pl.BlockSpec(memory_space=pltpu.VMEM)] * 3,
        scratch_shapes=[
            vmem((3, *block), BF16),
            vmem(block, BF16),
            vmem(weight.shape[::-1], BF16),
            vmem((3, *block), BF16),
            vmem((grid_rows, 768), BF16),
            vmem((grid_rows, 768), BF16),
            vmem((384, 768), BF16),
            vmem((768, 384), BF16),
            vmem((2, m // 2, n, wide, padded, 128), BF16),
            vmem((m // 2, n, wide, padded, 128), BF16),
            vmem((m // 2, n, wide, padded, 128), BF16),
            vmem((n - 1, m // 2, wide, padded, 128), BF16),
            vmem((m // 2, wide, padded, 128), BF16),
            vmem((m // 2 - 1, wide, padded, 128), BF16),
            dma((3,)), dma((2, 2)), dma((2, 2)), dma((2, 2)), dma((2, 2)),
            dma((2,)), dma((2,)), dma((2, n - 1)), dma((2, n - 1)),
            dma((m // 2 - 1,)), dma((m // 2 - 1,)),
        ],
        compiler_params=pltpu.CompilerParams(
            collective_id=0, has_side_effects=True, vmem_limit_bytes=32 * 1024 * 1024
        ),
    )(*(pltpu.with_memory_space_constraint(x, pltpu.HBM) for x in (volume, weight.T, cotangent)))
    activation, input_grad, weight_grad = pl.pallas_call(
        place,
        out_shape=tuple(jax.ShapeDtypeStruct(r.shape, r.dtype) for r in results),
        in_specs=[pl.BlockSpec(memory_space=pl.ANY)] * 3,
        out_specs=[pl.BlockSpec(memory_space=pl.ANY)] * 3,
        scratch_shapes=[dma((3,))],
        compiler_params=pltpu.CompilerParams(vmem_limit_bytes=1024 * 1024),
    )(*results)
    return activation, input_grad, weight_grad.T


def solution(mesh):
    return jax.shard_map(
        per_device,
        mesh=mesh,
        in_specs=(P("gz", "dp", None, None), P(), P("gz", "dp", None, None)),
        out_specs=(P("gz", "dp", None, None), P("gz", "dp", None, None), P("gz", "dp")),
        check_vma=False,
    )
```

```python
import functools
import math

import jax
import jax.numpy as jnp
from jax import lax
from jax.experimental import pallas as pl
from jax.experimental.pallas import tpu as pltpu
from jax.sharding import PartitionSpec as P

MESH = pl.DeviceIdType.MESH
BF16 = jnp.bfloat16
F32 = jnp.float32


def rolled(x, shift, axis):
    return pltpu.roll(x, shift % x.shape[axis], axis)


def pair_rows(plane, height, pairs):
    return jnp.concatenate([plane[:, 128 * k : 128 * (k + 1)] for k in range(pairs)], axis=0)


def windows(buf, a, height, low, high):
    zero = jnp.zeros((height, 128), buf.dtype)
    count = buf.shape[2] // 128

    def column(k):
        return buf[a, :, 128 * k : 128 * (k + 1)] if 0 <= k < count else zero

    own, after, before = (
        jnp.concatenate([column(k + shift) for k in range(low, high)], axis=0)
        for shift in (0, 1, -1)
    )
    lane = lax.broadcasted_iota(jnp.int32, own.shape, 1)
    return own, jnp.where(lane < 64, after, before)


def y_sum(parts, height):
    row = lax.broadcasted_iota(jnp.int32, (parts.shape[0], 128), 0) % height
    low = jnp.where(row == 0, 0.0, rolled(parts[:, 0:128], 1, 0))
    high = jnp.where(row == height - 1, 0.0, rolled(parts[:, 256:384], -1, 0))
    return parts[:, 128:256] + low + high


def kernel(
    geom, v_ref, w_ref, g_ref, act_ref, ig_ref, wg_ref,
    vbuf, gbuf, wbuf, dbuf, win, dwin, wfwd, wbwd,
    pack0, recv0, sum0, recv1, sum1, recv2,
    local_sem, vsend, vrecv, dsend, drecv, ssend0, srecv0, ssend1, srecv1, ssend2, srecv2,
):
    n, m, height, pairs, rows_out, cols_out, wide, scale = geom
    me = lax.axis_index("dp")
    my = lax.axis_index("gz")
    mz = m // 2
    z, core = lax.div(my, 2), lax.rem(my, 2)
    partner = my + 1 - 2 * core
    z_peers = [2 * lax.rem(z + k, mz) + core for k in range(1, mz)]

    barrier = pltpu.get_barrier_semaphore()
    for k in range(1, n):
        pl.semaphore_signal(
            barrier, inc=1, device_id={"dp": lax.rem(me + k, n)}, device_id_type=MESH
        )
    for peer in [partner] + z_peers:
        pl.semaphore_signal(barrier, inc=1, device_id={"gz": peer}, device_id_type=MESH)
    load_w = pltpu.make_async_copy(w_ref, wbuf, local_sem.at[0])
    load_v = pltpu.make_async_copy(v_ref.at[0, 0], vbuf.at[1], local_sem.at[1])
    load_g = pltpu.make_async_copy(g_ref.at[0, 0], gbuf, local_sem.at[2])
    load_w.start()
    load_v.start()
    load_g.start()
    pl.semaphore_wait(barrier, n + mz - 1)

    def halo(source, buf, ssem, rsem, piece, low, high):
        up = pltpu.make_async_remote_copy(
            src_ref=source.at[:, low:high], dst_ref=buf.at[0, :, low:high],
            send_sem=ssem.at[piece, 0], recv_sem=rsem.at[piece, 0],
            device_id={"dp": lax.rem(me + 1, n)}, device_id_type=MESH,
        )
        down = pltpu.make_async_remote_copy(
            src_ref=source.at[:, low:high], dst_ref=buf.at[2, :, low:high],
            send_sem=ssem.at[piece, 1], recv_sem=rsem.at[piece, 1],
            device_id={"dp": lax.rem(me + n - 1, n)}, device_id_type=MESH,
        )

        @pl.when(me < n - 1)
        def _():
            up.start()

        @pl.when(me > 0)
        def _():
            down.start()

        return up, down, buf, low, high

    def halo_arrive(up, down, buf, low, high):
        @pl.when(me > 0)
        def _():
            up.wait_recv()

        @pl.when(me == 0)
        def _():
            buf[0, :, low:high] = jnp.zeros((height, high - low), buf.dtype)

        @pl.when(me < n - 1)
        def _():
            down.wait_recv()

        @pl.when(me == n - 1)
        def _():
            buf[2, :, low:high] = jnp.zeros((height, high - low), buf.dtype)

    def halo_sent(up, down, *_):
        @pl.when(me < n - 1)
        def _():
            up.wait_send()

        @pl.when(me > 0)
        def _():
            down.wait_send()

    half = pairs // 2
    cut = 128 * (half + 1)
    v_halos = [
        halo(v_ref.at[0, 0], vbuf, vsend, vrecv, piece, low, high)
        for piece, (low, high) in enumerate(((0, cut), (cut, 128 * pairs)))
    ]

    load_w.wait()
    zero = jnp.zeros((64, 64), BF16)
    for a in range(3):
        for b in range(3):
            base = (a * 9 + b * 3) * 64
            k0, k1, k2 = (wbuf[:, base + 64 * c : base + 64 * (c + 1)] for c in range(3))
            top = jnp.concatenate([k1, k2, zero, k0], axis=1)
            bottom = jnp.concatenate([k0, k1, k2, zero], axis=1)
            wfwd[128 * b : 128 * (b + 1), 256 * a : 256 * (a + 1)] = jnp.concatenate(
                [top, bottom], axis=0
            )

    for a in range(3):
        for b in range(3):
            base = (a * 9 + b * 3) * 64
            k0, k1, k2 = (wbuf[:, base + 64 * c : base + 64 * (c + 1)] for c in range(3))
            left = jnp.concatenate([k1, k0, zero, k2], axis=0)
            right = jnp.concatenate([k2, k1, k0, zero], axis=0)
            fa, fb = 2 - a, 2 - b
            wbwd[256 * fa : 256 * (fa + 1), 128 * fb : 128 * (fb + 1)] = jnp.concatenate(
                [left, right], axis=1
            )

    def fill(target, buf, a, low, high):
        own, edge = windows(buf, a, height, low, high)
        target[height * low : height * high, 256 * a : 256 * a + 128] = own
        target[height * low : height * high, 256 * a + 128 : 256 * (a + 1)] = edge

    def plane_fwd(a, rows):
        return lax.dot_general(
            win[rows, 256 * a : 256 * (a + 1)], wfwd[:, 256 * a : 256 * (a + 1)],
            (((1,), (1,)), ((), ())), preferred_element_type=F32,
        )

    load_v.wait()
    fill(win, vbuf, 1, 0, pairs)
    halves = ((0, half), (half, pairs))
    middle = [plane_fwd(1, slice(height * low, height * high)) for low, high in halves]
    load_g.wait()
    deltas, d_halos, acts = [], [], []
    for piece, (low, high) in enumerate(halves):
        rows = slice(height * low, height * high)
        halo_arrive(*v_halos[piece])
        fill(win, vbuf, 0, low, high)
        fill(win, vbuf, 2, low, high)
        parts = middle[piece] + plane_fwd(0, rows) + plane_fwd(2, rows)
        pre = y_sum(parts, height)
        sig = 1.0 / (1.0 + jnp.exp(-pre))
        cot = pair_rows(gbuf[:, 128 * low : 128 * high], height, high - low).astype(F32)
        delta = (cot * sig * (1.0 + pre * (1.0 - sig))).astype(BF16)
        for k in range(low, high):
            at = slice(height * (k - low), height * (k - low + 1))
            dbuf[1, :, 128 * k : 128 * (k + 1)] = delta[at]
        d_halos.append(
            halo(dbuf.at[1], dbuf, dsend, drecv, piece, 128 * low, 128 * high)
        )
        acts.append((pre * sig).astype(BF16))
        deltas.append(delta)
    delta = jnp.concatenate(deltas, axis=0)

    wide_delta = delta.astype(F32)
    row = lax.broadcasted_iota(jnp.int32, wide_delta.shape, 0) % height
    ahead = jnp.where(row == height - 1, 0.0, rolled(wide_delta, -1, 0)).astype(BF16)
    behind = jnp.where(row == 0, 0.0, rolled(wide_delta, 1, 0)).astype(BF16)
    moved = jnp.concatenate([ahead, delta, behind], axis=1)
    lane = lax.broadcasted_iota(jnp.int32, (64, 128), 1) < 64
    early = mz
    parts_z = ((0, mz),)
    zero_copies = []
    gathered = []
    lanes = lax.broadcasted_iota(jnp.int32, (64, 128), 1)

    def weight_terms(planes, low_z, high_z, stage):
        span = win[:, 256 * planes[0] : 256 * (planes[-1] + 1)]
        terms = lax.dot_general(
            moved, span, (((0,), (0,)), ((), ())), preferred_element_type=F32
        )
        quads = []
        for p in range(len(planes)):
            for b in range(3):
                first = terms[128 * b : 128 * b + 64, 256 * p : 256 * (p + 1)]
                second = terms[128 * b + 64 : 128 * (b + 1), 256 * p : 256 * (p + 1)]
                quads.append((first[:, :128], first[:, 128:], second[:, :128], second[:, 128:]))
        out_tiles = []
        for q in range(0, len(quads), 2):
            a1, a2, b1, b2 = quads[q]
            out_tiles.append(rolled(jnp.where(lane, a1, a2), 64, 1) + b1)
            third = rolled(a1, 64, 1) + b2
            if q + 1 == len(quads):
                out_tiles.append(jnp.where(lane, third, 0.0))
                continue
            c1, c2, e1, e2 = quads[q + 1]
            out_tiles.append(jnp.where(lane, third, c2 + rolled(e1, 64, 1)))
            out_tiles.append(c1 + rolled(jnp.where(lane, e2, e1), 64, 1))
        gathered.extend(tile * scale for tile in out_tiles)
        for g in range(2 * low_z, 2 * high_z):
            start, offset = (g * rows_out) // 128, (g * rows_out) % 128
            for j in range(wide):
                tile = gathered[start + j]
                if offset:
                    tile = rolled(tile, -offset, 1)
                    if (g + 1) * rows_out > 128 * (start + j + 1):
                        after = rolled(gathered[start + j + 1], -offset, 1)
                        tile = jnp.where(lanes < 128 - offset, tile, after)
                tile = tile.astype(BF16)
                for d in range(n):
                    part = tile[cols_out * d : cols_out * (d + 1)]
                    if cols_out % 16:
                        fill_rows = jnp.zeros((pack0.shape[4] - cols_out, 128), BF16)
                        part = jnp.concatenate([part, fill_rows], axis=0)
                    pack0[g % 2, g // 2, d, j] = part
        copy = pltpu.make_async_remote_copy(
            src_ref=pack0.at[1 - core, low_z:high_z], dst_ref=recv0.at[low_z:high_z],
            send_sem=ssend0.at[stage], recv_sem=srecv0.at[stage],
            device_id={"gz": partner}, device_id_type=MESH,
        )
        copy.start()
        zero_copies.append(copy)

    weight_terms((0, 1, 2), 0, mz, 0)

    first_copies = []
    for stage, (low_z, high_z) in enumerate(parts_z):
        zero_copies[stage].wait_recv()
        both = pack0[core, low_z:high_z].astype(F32) + recv0[low_z:high_z].astype(F32)
        sum0[low_z:high_z] = both.astype(BF16)
        copies = []
        for k in range(1, n):
            peer = lax.rem(me + k, n)
            copy = pltpu.make_async_remote_copy(
                src_ref=sum0.at[low_z:high_z, peer], dst_ref=recv1.at[k - 1, low_z:high_z],
                send_sem=ssend1.at[stage, k - 1], recv_sem=srecv1.at[stage, k - 1],
                device_id={"dp": peer}, device_id_type=MESH,
            )
            copy.start()
            copies.append(copy)
        first_copies.append(copies)

    for (low, high), act in zip(halves, acts):
        for k in range(low, high):
            at = slice(height * (k - low), height * (k - low + 1))
            act_ref[0, 0, :, 128 * k : 128 * (k + 1)] = act[at]
    fill(dwin, dbuf, 1, 0, pairs)
    back = jnp.dot(dwin[:, 256:512], wbwd[256:512, :], preferred_element_type=F32)
    second_copies = []
    for k in range(1, mz):
        second_copies.append(pltpu.make_async_remote_copy(
            src_ref=sum1.at[lax.rem(z + k, mz)], dst_ref=recv2.at[k - 1],
            send_sem=ssend2.at[k - 1], recv_sem=srecv2.at[k - 1],
            device_id={"gz": z_peers[k - 1]}, device_id_type=MESH,
        ))
    for stage, (low_z, high_z) in enumerate(parts_z):
        total = sum0[low_z:high_z, me].astype(F32)
        for k in range(1, n):
            first_copies[stage][k - 1].wait_recv()
            total = total + recv1[k - 1, low_z:high_z].astype(F32)
        sum1[low_z:high_z] = total.astype(BF16)
        for k in range(1, mz):
            target = lax.rem(z + k, mz)

            @pl.when((target < early) if stage == 0 else (target >= early))
            def _(copy=second_copies[k - 1]):
                copy.start()

    for piece in d_halos:
        halo_arrive(*piece)
    for a in (0, 2):
        fill(dwin, dbuf, a, 0, pairs)
        back = back + jnp.dot(
            dwin[:, 256 * a : 256 * (a + 1)], wbwd[256 * a : 256 * (a + 1), :],
            preferred_element_type=F32,
        )
    grad = y_sum(back, height).astype(BF16)
    for k in range(pairs):
        ig_ref[0, 0, :, 128 * k : 128 * (k + 1)] = grad[height * k : height * (k + 1)]

    for piece in v_halos + d_halos:
        halo_sent(*piece)
    for copy in zero_copies + first_copies[0]:
        copy.wait_send()
    total = sum1[z].astype(F32)
    for k in range(1, mz):
        second_copies[k - 1].wait_recv()
        total = total + recv2[k - 1].astype(F32)
    for t in range(wide):
        count = min(128, rows_out - 128 * t)
        wg_ref[:, 128 * t : 128 * t + count] = total[t, :cols_out, :count]
    for copy in second_copies:
        copy.wait_send()


def place(a_ref, i_ref, w_ref, act_ref, ig_ref, wg_ref, sem):
    pairs = ((a_ref, act_ref), (i_ref, ig_ref), (w_ref, wg_ref))
    copies = [pltpu.make_async_copy(a, b, sem.at[k]) for k, (a, b) in enumerate(pairs)]
    for copy in copies:
        copy.start()
    for copy in copies:
        copy.wait()


def per_device(volume, weight, cotangent):
    n = lax.axis_size("dp")
    m = lax.axis_size("gz")
    chans = weight.shape[1]
    universes, planes, height, merged = volume.shape
    assert chans == 64 and universes == 1 and planes == 1
    pairs = merged // 128
    cells = height * pairs * 2
    rows_out = weight.shape[0] // m
    cols_out = chans // n
    padded = -(-cols_out // 16) * 16
    wide = -(-rows_out // 128)
    assert 27 * 64 == weight.shape[0]
    scale = 1.0 / math.sqrt(n * m * cells)
    geom = (n, m, height, pairs, rows_out, cols_out, wide, scale)
    vmem = pltpu.VMEM
    dma = pltpu.SemaphoreType.DMA
    block = (height, merged)
    grid_rows = pairs * height
    results = pl.pallas_call(
        functools.partial(kernel, geom),
        out_shape=(
            vmem(volume.shape, BF16),
            vmem(volume.shape, BF16),
            vmem((cols_out, rows_out), F32),
        ),
        in_specs=[pl.BlockSpec(memory_space=pltpu.HBM)] * 3,
        out_specs=[pl.BlockSpec(memory_space=pltpu.VMEM)] * 3,
        scratch_shapes=[
            vmem((3, *block), BF16),
            vmem(block, BF16),
            vmem(weight.shape[::-1], BF16),
            vmem((3, *block), BF16),
            vmem((grid_rows, 768), BF16),
            vmem((grid_rows, 768), BF16),
            vmem((384, 768), BF16),
            vmem((768, 384), BF16),
            vmem((2, m // 2, n, wide, padded, 128), BF16),
            vmem((m // 2, n, wide, padded, 128), BF16),
            vmem((m // 2, n, wide, padded, 128), BF16),
            vmem((n - 1, m // 2, wide, padded, 128), BF16),
            vmem((m // 2, wide, padded, 128), BF16),
            vmem((m // 2 - 1, wide, padded, 128), BF16),
            dma((3,)), dma((2, 2)), dma((2, 2)), dma((2, 2)), dma((2, 2)),
            dma((2,)), dma((2,)), dma((2, n - 1)), dma((2, n - 1)),
            dma((m // 2 - 1,)), dma((m // 2 - 1,)),
        ],
        compiler_params=pltpu.CompilerParams(
            collective_id=0, has_side_effects=True, vmem_limit_bytes=32 * 1024 * 1024
        ),
    )(*(pltpu.with_memory_space_constraint(x, pltpu.HBM) for x in (volume, weight.T, cotangent)))
    activation, input_grad, weight_grad = pl.pallas_call(
        place,
        out_shape=tuple(jax.ShapeDtypeStruct(r.shape, r.dtype) for r in results),
        in_specs=[pl.BlockSpec(memory_space=pl.ANY)] * 3,
        out_specs=[pl.BlockSpec(memory_space=pl.ANY)] * 3,
        scratch_shapes=[dma((3,))],
        compiler_params=pltpu.CompilerParams(vmem_limit_bytes=1024 * 1024),
    )(*results)
    return activation, input_grad, weight_grad.T


def solution(mesh):
    return jax.shard_map(
        per_device,
        mesh=mesh,
        in_specs=(P("gz", "dp", None, None), P(), P("gz", "dp", None, None)),
        out_specs=(P("gz", "dp", None, None), P("gz", "dp", None, None), P("gz", "dp")),
        check_vma=False,
    )
```
